512 devices in a mesh: rep: 16 (over x, z_hi, core), fsdp: 32 (over y, z_lo).
Axes of the slice: x: 4, y: 4, z: 16 (z_hi: 2, z_lo: 8; z = z_hi * 8 + z_lo), core: 2. Of those that a mesh axis runs over, the one named last changes fastest.
Arguments:
- inner: bfloat16 [16, 1, 8192, 2048], P('rep', None, 'fsdp'), may hold values from -6 to 6
- anchor: bfloat16 [1, 8192, 2048], P(None, 'fsdp'), may hold values from -6 to 6
- exponent: int32 [16, 1, 8192, 64], P('rep', None, 'fsdp'), may hold values from -1 to 1
- momentum: float32 [1, 8192, 2048], P(None, 'fsdp', 'rep'), may hold values from -4 to 4
Outputs:
- mixed: bfloat16 [16, 1, 8192, 2048], P('rep', None, 'fsdp')
- new_anchor: bfloat16 [1, 8192, 2048], P(None, 'fsdp')
- momentum_next: float32 [1, 8192, 2048], P(None, 'fsdp', 'rep')
The draws below stay inside these ranges and needn't reach their ends.
All inputs are finite; a program needn't handle non-finite values.
Results may differ from the reference program's by a relative error of at most 0.0035.
Values may be sent and summed in bfloat16 or wider, within the bound.
A program may use at most 64 MiB of HBM per device.

```python
import jax
import jax.numpy as jnp
from jax import lax

D = 8192
KVW = 2048
LAYERS = 1
REPS = 16


def with_ends(entries, key, low, top_value):
    place = [jax.random.randint(jax.random.fold_in(key, axis), (), 0, length) for axis, length in enumerate(entries.shape)]
    main_axis = entries.shape.index(max(entries.shape))
    beside = place[:main_axis] + [(place[main_axis] + 1) % entries.shape[main_axis]] + place[main_axis + 1:]
    return entries.at[tuple(place)].set(low).at[tuple(beside)].set(top_value)


def steps_of(rng, extent, cuts, low, largest):
    def one(axis_at, parts):
        steps = jax.random.uniform(jax.random.fold_in(jax.random.fold_in(rng, 6), axis_at), (parts,), jnp.float32, low / len(cuts), largest / len(cuts))
        return jnp.repeat(jnp.exp(steps), extent[axis_at] // parts).reshape((-1,) + (1,) * (len(extent) - axis_at - 1))

    factor_of = one(*cuts[0])
    for cut in cuts[1:]:
        factor_of = factor_of * one(*cut)
    return factor_of


def gaussian(key, shape, deviation, limit, pieces=(), dtype=jnp.bfloat16):
    values = jax.random.normal(key, shape, jnp.float32) * deviation
    if len(pieces) > 0:
        values = steps_of(key, shape, pieces, -0.22, 0.18) * values
    return jnp.clip(values, min=-limit, max=limit).astype(dtype)


def setup_inputs(seed: int = 0) -> dict:
    streams_of = jax.random.split(jax.random.key(seed), 5)
    return {
        "inner": gaussian(streams_of[0], (REPS, LAYERS, D, KVW), 1.0, 6.0, ((0, 16), (2, 32))),
        "anchor": gaussian(streams_of[1], (LAYERS, D, KVW), 1.0, 6.0, ((1, 32),)),
        "exponent": with_ends(jax.random.randint(streams_of[2], (REPS, LAYERS, D, KVW // 32), -1, 2), jax.random.fold_in(streams_of[2], 1), -1, 1).astype(jnp.int32),
        "momentum": gaussian(streams_of[3], (LAYERS, D, KVW), 0.5, 4.0, ((1, 32), (2, 16)), jnp.float32),
    }


levels_table = ((0.25, 0.5), (0.75, 0.5), (1.25, 0.5), (1.75, 0.5), (2.5, 1.0), (3.5, 1.0), (5.0, 2.0))


def block_scale(exponent):
    scale = jnp.zeros(exponent.shape, jnp.float32)
    for power in (-1, 0, 1):
        scale = scale + jnp.where(exponent == power, jnp.float32(2.0 ** power), jnp.float32(0.0))
    return scale


def encode(delta, exponent):
    shape = delta.shape
    blocks = delta.reshape(shape[:-1] + (shape[-1] // 32, 32))
    scale = block_scale(exponent)[..., None]
    magnitude = jnp.abs(blocks) / scale
    level = jnp.zeros(blocks.shape, jnp.float32)
    for bound, height in levels_table:
        level = level + jnp.where(magnitude >= bound, jnp.float32(height), jnp.float32(0.0))
    signed = jnp.where(blocks < 0, -level, level) * scale
    return signed.reshape(shape).astype(jnp.bfloat16)


def reference(inner, anchor, exponent, momentum):
    anchor_wide = anchor.astype(jnp.float32)

    def accumulate(total, pair):
        weights, powers = pair
        delta = anchor_wide - weights.astype(jnp.float32)
        return total + encode(delta, powers).astype(jnp.float32), None

    total, _ = lax.scan(accumulate, jnp.zeros(anchor.shape, jnp.float32), (inner, exponent))
    outer_grad = total / REPS
    momentum_next = 0.9 * momentum + outer_grad
    new_anchor = (anchor_wide - 0.7 * (outer_grad + 0.9 * momentum_next)).astype(jnp.bfloat16)
    mixed = (0.5 * inner.astype(jnp.float32) + 0.5 * new_anchor.astype(jnp.float32)[None]).astype(jnp.bfloat16)
    return mixed, new_anchor, momentum_next
```

```python
import functools

import jax
import jax.numpy as jnp
from jax import lax
from jax.experimental import pallas as pl
from jax.experimental.pallas import tpu as pltpu
from jax.sharding import PartitionSpec as P

MESH = pl.DeviceIdType.MESH
BLOCK = 32
LANE = 128
TILE = 16
GROUP = 8
REPS = 16
MINE, OTHER = 0.5, 0.7 * 1.9 / REPS
BOUNDS = ((0.25, 0.5), (0.75, 1.0), (1.25, 1.5), (1.75, 2.0), (2.5, 3.0), (3.5, 4.0), (5.0, 6.0))
CHUNKS = (4, 4, 4, 4)
PEERS = tuple((dx, dc) for dx in range(4) for dc in range(2) if (dx, dc) != (0, 0))


def column_of(group, half):
    return ((group // 2) * 4 + half * 2 + group % 2) * LANE


def spans():
    first = 0
    for k, tiles in enumerate(CHUNKS):
        yield k, first, tiles
        first += tiles


def exchange(
    inner,
    anchor,
    exponent,
    momentum,
    gathered,
    momentum_next,
    inner_v,
    anchor_v,
    exponent_v,
    spread,
    scale_v,
    inverse_v,
    coded,
    arrived,
    own_sum,
    z_out,
    z_in,
    load_sem,
    small_sem,
    rs_send,
    rs_recv,
    z_send,
    z_recv,
    ag_send,
    ag_recv,
    momentum_v,
):
    rep, fsdp = lax.axis_index("rep"), lax.axis_index("fsdp")
    x, half, core = rep // 4, (rep // 2) % 2, rep % 2
    group = x * 2 + core
    own_column = pl.multiple_of(rep * LANE, LANE)
    other_column = pl.multiple_of((x * 4 + (1 - half) * 2 + core) * LANE, LANE)

    def place(dx, dc):
        px, pc = lax.rem(x + dx, 4), lax.rem(core + dc, 2)
        return px * 2 + pc, (px * 4 + half * 2 + pc, fsdp)

    across = (x * 4 + (1 - half) * 2 + core, fsdp)

    barrier = pltpu.get_barrier_semaphore()
    for peer in PEERS:
        pl.semaphore_signal(barrier, inc=1, device_id=place(*peer)[1], device_id_type=MESH)
    pl.semaphore_signal(barrier, inc=1, device_id=across, device_id_type=MESH)

    small = [
        pltpu.make_async_copy(exponent, exponent_v, small_sem.at[0]),
        pltpu.make_async_copy(momentum, momentum_v, small_sem.at[1]),
    ]
    small[0].start()
    loads = []
    for k, first, tiles in spans():
        rows = pl.ds(first * TILE, tiles * TILE)
        pair = (
            pltpu.make_async_copy(inner.at[rows], inner_v.at[rows], load_sem.at[k, 0]),
            pltpu.make_async_copy(anchor.at[rows], anchor_v.at[rows], load_sem.at[k, 1]),
        )
        for copy in pair:
            copy.start()
        loads.append(pair)
    small[1].start()

    width = anchor.shape[1]
    blocks = width // BLOCK
    block_of = lax.broadcasted_iota(jnp.int32, (blocks, width), 1) // BLOCK
    row_of = lax.broadcasted_iota(jnp.int32, (blocks, width), 0)
    spread[...] = jnp.where(block_of == row_of, 1.0, 0.0).astype(jnp.bfloat16)
    small[0].wait()

    for k, first, tiles in spans():
        rows = pl.ds(first * TILE, tiles * TILE)
        powers = exponent_v[rows, :]
        scale, inverse = jnp.zeros(powers.shape, jnp.float32), jnp.zeros(powers.shape, jnp.float32)
        for power in (-1, 0, 1):
            scale = jnp.where(powers == power, jnp.float32(2.0**power), scale)
            inverse = jnp.where(powers == power, jnp.float32(2.0**-power), inverse)
        for value, target in ((scale, scale_v), (inverse, inverse_v)):
            target[rows, :] = jnp.dot(
                value.astype(jnp.bfloat16), spread[...], preferred_element_type=jnp.float32
            )
        for copy in loads[k]:
            copy.wait()

        def code(tile, carry):
            rows = pl.ds(pl.multiple_of(tile * TILE, TILE), TILE)
            for g in range(GROUP):
                for h in range(2):
                    columns = pl.ds(column_of(g, h), LANE)
                    delta = anchor_v[rows, columns].astype(jnp.float32) - inner_v[
                        rows, columns
                    ].astype(jnp.float32)
                    magnitude = jnp.abs(delta) * inverse_v[rows, columns]
                    scale = scale_v[rows, columns]
                    level = jnp.zeros(delta.shape, jnp.float32)
                    for bound, height in BOUNDS:
                        level = jnp.where(magnitude >= bound, jnp.float32(height), level)
                    level = level * jnp.where(delta < 0, -scale, scale)
                    coded[g, tile, h] = level.astype(jnp.bfloat16)
            return carry

        lax.fori_loop(first, first + tiles, code, 0)

    pl.semaphore_wait(barrier, len(PEERS) + 1)

    def start(source, destination, send, recv, device):
        pltpu.make_async_remote_copy(
            src_ref=source,
            dst_ref=destination,
            send_sem=send,
            recv_sem=recv,
            device_id=device,
            device_id_type=MESH,
        ).start()

    def wait(buffer, semaphore):
        pltpu.make_async_copy(buffer, buffer, semaphore).wait()

    for k, first, tiles in spans():
        span = pl.ds(first, tiles)
        for slot, peer in enumerate(PEERS):
            there, device = place(*peer)
            start(
                coded.at[there, span], arrived.at[slot, span], rs_send.at[k], rs_recv.at[k], device
            )

    small[1].wait()
    for k, first, tiles in spans():
        span = pl.ds(first, tiles)
        wait(arrived.at[:, span], rs_recv.at[k])

        def add(tile, carry):
            rows = pl.ds(pl.multiple_of(tile * TILE, TILE), TILE)
            own = coded[group, tile, half].astype(jnp.float32)
            other = coded[group, tile, 1 - half].astype(jnp.float32)
            for slot in range(len(PEERS)):
                own = own + arrived[slot, tile, half].astype(jnp.float32)
                other = other + arrived[slot, tile, 1 - half].astype(jnp.float32)
            anchor_own = anchor_v[rows, pl.ds(own_column, LANE)].astype(jnp.float32)
            mine = MINE * anchor_own - OTHER * own - (0.7 * 0.81) * momentum_v[rows, :]
            own_sum[rows, :] = own
            z_out[tile, 0] = mine.astype(jnp.bfloat16)
            z_out[tile, 1] = other.astype(jnp.bfloat16)
            return carry

        lax.fori_loop(first, first + tiles, add, 0)
        start(z_out.at[span], z_in.at[span], z_send.at[k], z_recv.at[k], across)

    for k, first, tiles in spans():
        span = pl.ds(first, tiles)
        wait(z_in.at[span], z_recv.at[k])

        def update(tile, carry):
            rows = pl.ds(pl.multiple_of(tile * TILE, TILE), TILE)

            def new(column, part, sums):
                wide = anchor_v[rows, pl.ds(column, LANE)].astype(jnp.float32)
                rest = (1.0 - MINE) * wide - OTHER * sums.astype(jnp.float32)
                return (part.astype(jnp.float32) + rest).astype(jnp.bfloat16)

            theirs = z_in[tile, 1]
            gathered[group, tile, half] = new(own_column, z_out[tile, 0], theirs)
            gathered[group, tile, 1 - half] = new(other_column, z_in[tile, 0], z_out[tile, 1])
            outer_grad = (own_sum[rows, :] + theirs.astype(jnp.float32)) * (1.0 / REPS)
            momentum_next[rows, :] = 0.9 * momentum_v[rows, :] + outer_grad
            return carry

        lax.fori_loop(first, first + tiles, update, 0)
        for slot, peer in enumerate(PEERS):
            _, device = place(*peer)
            piece = gathered.at[group, span]
            start(piece, piece, ag_send.at[k], ag_recv.at[k], device)

    for k, first, tiles in spans():
        span = pl.ds(first, tiles)
        wait(arrived.at[:, span], rs_send.at[k])
        wait(z_out.at[span], z_send.at[k])
    for k, first, tiles in spans():
        span = pl.ds(first, tiles)
        wait(arrived.at[:, span], ag_recv.at[k])
        wait(arrived.at[:, span], ag_send.at[k])


def mix(inner, gathered, momentum_in, mixed, new_anchor, momentum_out):
    for t in range(gathered.shape[1]):
        rows = pl.ds(t * TILE, TILE)
        for g in range(GROUP):
            for h in range(2):
                columns = pl.ds(column_of(g, h), LANE)
                new = gathered[g, t, h]
                new_anchor[rows, columns] = new
                mixed[rows, columns] = (
                    0.5 * inner[rows, columns].astype(jnp.float32) + 0.5 * new.astype(jnp.float32)
                ).astype(jnp.bfloat16)
    momentum_out[...] = momentum_in[...]


def on_device(inner, anchor, exponent, momentum):
    rows, width = anchor.shape[1:]
    tiles = rows // TILE
    blocks = exponent.shape[-1]
    inner2 = inner.reshape(rows, width)
    chunks = len(CHUNKS)
    anywhere = pl.BlockSpec(memory_space=pl.ANY)
    inside = pl.BlockSpec(memory_space=pltpu.VMEM)
    dma = pltpu.SemaphoreType.DMA
    gathered, momentum_next = pl.pallas_call(
        exchange,
        out_shape=(
            jax.ShapeDtypeStruct((GROUP, tiles, 2, TILE, LANE), jnp.bfloat16),
            jax.ShapeDtypeStruct((rows, LANE), jnp.float32),
        ),
        in_specs=[anywhere] * 4,
        out_specs=(inside, inside),
        scratch_shapes=[
            pltpu.VMEM((rows, width), jnp.bfloat16),
            pltpu.VMEM((rows, width), jnp.bfloat16),
            pltpu.VMEM((rows, blocks), jnp.int32),
            pltpu.VMEM((blocks, width), jnp.bfloat16),
            pltpu.VMEM((rows, width), jnp.float32),
            pltpu.VMEM((rows, width), jnp.float32),
            pltpu.VMEM((GROUP, tiles, 2, TILE, LANE), jnp.bfloat16),
            pltpu.VMEM((len(PEERS), tiles, 2, TILE, LANE), jnp.bfloat16),
            pltpu.VMEM((rows, LANE), jnp.float32),
            pltpu.VMEM((tiles, 2, TILE, LANE), jnp.bfloat16),
            pltpu.VMEM((tiles, 2, TILE, LANE), jnp.bfloat16),
            dma((chunks, 2)),
            dma((2,)),
            dma((chunks,)),
            dma((chunks,)),
            dma((chunks,)),
            dma((chunks,)),
            dma((chunks,)),
            dma((chunks,)),
            pltpu.VMEM((rows, LANE), jnp.float32),
        ],
        compiler_params=pltpu.CompilerParams(
            collective_id=0, has_side_effects=True, vmem_limit_bytes=24 << 20
        ),
        name="exchange",
    )(
        inner2,
        anchor.reshape(rows, width),
        exponent.reshape(rows, blocks),
        momentum.reshape(rows, LANE),
    )

    steps = 4
    part = rows // steps
    wide = pl.BlockSpec((part, width), lambda i: (i, 0))
    narrow = pl.BlockSpec((part, LANE), lambda i: (i, 0))
    mixed, new_anchor, momentum_next = pl.pallas_call(
        mix,
        out_shape=(
            jax.ShapeDtypeStruct((rows, width), jnp.bfloat16),
            jax.ShapeDtypeStruct((rows, width), jnp.bfloat16),
            jax.ShapeDtypeStruct((rows, LANE), jnp.float32),
        ),
        grid=(steps,),
        in_specs=[
            wide,
            pl.BlockSpec((GROUP, part // TILE, 2, TILE, LANE), lambda i: (0, i, 0, 0, 0)),
            narrow,
        ],
        out_specs=(wide, wide, narrow),
        compiler_params=pltpu.CompilerParams(vmem_limit_bytes=16 << 20),
        name="mix",
    )(inner2, gathered, momentum_next)
    return (
        mixed.reshape(inner.shape),
        new_anchor.reshape(anchor.shape),
        momentum_next.reshape(momentum.shape),
    )


def solution(mesh):
    return jax.shard_map(
        on_device,
        mesh=mesh,
        in_specs=(
            P("rep", None, "fsdp", None),
            P(None, "fsdp", None),
            P("rep", None, "fsdp", None),
            P(None, "fsdp", "rep"),
        ),
        out_specs=(P("rep", None, "fsdp", None), P(None, "fsdp", None), P(None, "fsdp", "rep")),
        check_vma=False,
    )
```

```python
import functools

import jax
import jax.numpy as jnp
from jax import lax
from jax.experimental import pallas as pl
from jax.experimental.pallas import tpu as pltpu
from jax.sharding import PartitionSpec as P

MESH = pl.DeviceIdType.MESH
BLOCK = 32
LANE = 128
TILE = 16
GROUP = 8
REPS = 16
MINE, OTHER = 0.5, 0.7 * 1.9 / REPS
BOUNDS = ((0.25, 0.5), (0.75, 1.0), (1.25, 1.5), (1.75, 2.0), (2.5, 3.0), (3.5, 4.0), (5.0, 6.0))
CHUNKS = (4, 4, 4, 4)
PEERS = tuple((dx, dc) for dx in range(4) for dc in range(2) if (dx, dc) != (0, 0))


def column_of(group, half):
    return ((group // 2) * 4 + half * 2 + group % 2) * LANE


def spans():
    first = 0
    for k, tiles in enumerate(CHUNKS):
        yield k, first, tiles
        first += tiles


def exchange(
    inner,
    anchor,
    exponent,
    momentum,
    gathered,
    momentum_next,
    inner_v,
    anchor_v,
    exponent_v,
    power_rows,
    spread,
    scale_v,
    inverse_v,
    coded,
    arrived,
    own_sum,
    z_out,
    z_in,
    load_sem,
    small_sem,
    rs_send,
    rs_recv,
    z_send,
    z_recv,
    ag_send,
    ag_recv,
    momentum_v,
    near_sem,
    far_sem,
):
    rep, fsdp = lax.axis_index("rep"), lax.axis_index("fsdp")
    x, half, core = rep // 4, (rep // 2) % 2, rep % 2
    group = x * 2 + core
    own_column = pl.multiple_of(rep * LANE, LANE)
    other_column = pl.multiple_of((x * 4 + (1 - half) * 2 + core) * LANE, LANE)

    def place(dx, dc):
        px, pc = lax.rem(x + dx, 4), lax.rem(core + dc, 2)
        return px * 2 + pc, (px * 4 + half * 2 + pc, fsdp)

    across = (x * 4 + (1 - half) * 2 + core, fsdp)

    partner = (x * 4 + half * 2 + 1 - core, fsdp)

    barrier = pltpu.get_barrier_semaphore()
    for dx in range(1, 4):
        hub = (lax.rem(x + dx, 4) * 4 + half * 2, fsdp)
        pl.semaphore_signal(barrier, inc=1, device_id=hub, device_id_type=MESH)

    @pl.when(core == 1)
    def _():
        pl.semaphore_signal(barrier, inc=1, device_id=partner, device_id_type=MESH)

    far = (x * 4 + (1 - half) * 2 + 1, fsdp)
    pl.semaphore_signal(barrier, inc=1, device_id=far, device_id_type=MESH)

    small = [
        pltpu.make_async_copy(exponent, exponent_v, small_sem.at[0]),
        pltpu.make_async_copy(momentum, momentum_v, small_sem.at[1]),
    ]
    small[0].start()
    loads = []
    for k, first, tiles in spans():
        rows = pl.ds(first * TILE, tiles * TILE)
        pair = (
            pltpu.make_async_copy(inner.at[rows], inner_v.at[rows], load_sem.at[k, 0]),
            pltpu.make_async_copy(anchor.at[rows], anchor_v.at[rows], load_sem.at[k, 1]),
        )
        for copy in pair:
            copy.start()
        loads.append(pair)
    small[1].start()

    width = anchor.shape[1]
    blocks = width // BLOCK
    block_of = lax.broadcasted_iota(jnp.int32, (blocks, width), 1) // BLOCK
    row_of = lax.broadcasted_iota(jnp.int32, (blocks, width), 0)
    spread[...] = jnp.where(block_of == row_of, 1.0, 0.0).astype(jnp.bfloat16)
    small[0].wait()
    power_rows[...] = exponent_v[...].T

    def start(source, destination, send, recv, device):
        pltpu.make_async_remote_copy(
            src_ref=source,
            dst_ref=destination,
            send_sem=send,
            recv_sem=recv,
            device_id=device,
            device_id_type=MESH,
        ).start()

    def wait(buffer, semaphore):
        pltpu.make_async_copy(buffer, buffer, semaphore).wait()

    for k, first, tiles in spans():
        rows = pl.ds(first * TILE, tiles * TILE)
        powers = power_rows[rows, :]
        scale, inverse = jnp.zeros(powers.shape, jnp.float32), jnp.zeros(powers.shape, jnp.float32)
        for power in (-1, 0, 1):
            scale = jnp.where(powers == power, jnp.float32(2.0**power), scale)
            inverse = jnp.where(powers == power, jnp.float32(2.0**-power), inverse)
        for value, target in ((scale, scale_v), (inverse, inverse_v)):
            target[rows, :] = jnp.dot(
                value.astype(jnp.bfloat16), spread[...], preferred_element_type=jnp.float32
            )
        for copy in loads[k]:
            copy.wait()

        def code(tile, carry):
            rows = pl.ds(pl.multiple_of(tile * TILE, TILE), TILE)
            for g in range(GROUP):
                for h in range(2):
                    columns = pl.ds(column_of(g, h), LANE)
                    delta = anchor_v[rows, columns].astype(jnp.float32) - inner_v[
                        rows, columns
                    ].astype(jnp.float32)
                    magnitude = jnp.abs(delta) * inverse_v[rows, columns]
                    scale = scale_v[rows, columns]
                    level = jnp.zeros(delta.shape, jnp.float32)
                    for bound, height in BOUNDS:
                        level = jnp.where(magnitude >= bound, jnp.float32(height), level)
                    level = level * jnp.where(delta < 0, -scale, scale)
                    coded[g, tile, h] = level.astype(jnp.bfloat16)
            return carry

        lax.fori_loop(first, first + tiles, code, 0)

        if k == 0:

            @pl.when(core == 0)
            def _():
                pl.semaphore_wait(barrier, len(PEERS))
                pl.semaphore_signal(near_sem, inc=1, device_id=partner, device_id_type=MESH)

            @pl.when(core == 1)
            def _():
                pl.semaphore_wait(near_sem, 1)

        span = pl.ds(first, tiles)
        for slot, peer in enumerate(PEERS):
            there, device = place(*peer)
            start(
                coded.at[there, span], arrived.at[slot, span], rs_send.at[k], rs_recv.at[k], device
            )

    @pl.when(core == 1)
    def _():
        pl.semaphore_wait(barrier, 2)
        pl.semaphore_signal(far_sem, inc=1, device_id=partner, device_id_type=MESH)

    @pl.when(core == 0)
    def _():
        pl.semaphore_wait(far_sem, 1)

    small[1].wait()
    for k, first, tiles in spans():
        span = pl.ds(first, tiles)
        wait(arrived.at[:, span], rs_recv.at[k])

        def add(tile, carry):
            rows = pl.ds(pl.multiple_of(tile * TILE, TILE), TILE)
            own = coded[group, tile, half].astype(jnp.float32)
            other = coded[group, tile, 1 - half].astype(jnp.float32)
            for slot in range(len(PEERS)):
                own = own + arrived[slot, tile, half].astype(jnp.float32)
                other = other + arrived[slot, tile, 1 - half].astype(jnp.float32)
            anchor_own = anchor_v[rows, pl.ds(own_column, LANE)].astype(jnp.float32)
            mine = MINE * anchor_own - OTHER * own - (0.7 * 0.81) * momentum_v[rows, :]
            own_sum[rows, :] = own
            z_out[tile, 0] = mine.astype(jnp.bfloat16)
            z_out[tile, 1] = other.astype(jnp.bfloat16)
            return carry

        lax.fori_loop(first, first + tiles, add, 0)
        start(z_out.at[span], z_in.at[span], z_send.at[k], z_recv.at[k], across)

    for k, first, tiles in spans():
        span = pl.ds(first, tiles)
        wait(z_in.at[span], z_recv.at[k])

        def update(tile, carry):
            rows = pl.ds(pl.multiple_of(tile * TILE, TILE), TILE)

            def new(column, part, sums):
                wide = anchor_v[rows, pl.ds(column, LANE)].astype(jnp.float32)
                rest = (1.0 - MINE) * wide - OTHER * sums.astype(jnp.float32)
                return (part.astype(jnp.float32) + rest).astype(jnp.bfloat16)

            theirs = z_in[tile, 1]
            gathered[group, tile, half] = new(own_column, z_out[tile, 0], theirs)
            gathered[group, tile, 1 - half] = new(other_column, z_in[tile, 0], z_out[tile, 1])
            outer_grad = (own_sum[rows, :] + theirs.astype(jnp.float32)) * (1.0 / REPS)
            momentum_next[rows, :] = 0.9 * momentum_v[rows, :] + outer_grad
            return carry

        lax.fori_loop(first, first + tiles, update, 0)
        for slot, peer in enumerate(PEERS):
            _, device = place(*peer)
            piece = gathered.at[group, span]
            start(piece, piece, ag_send.at[k], ag_recv.at[k], device)

    for k, first, tiles in spans():
        span = pl.ds(first, tiles)
        wait(arrived.at[:, span], rs_send.at[k])
        wait(z_out.at[span], z_send.at[k])
    for k, first, tiles in spans():
        span = pl.ds(first, tiles)
        wait(arrived.at[:, span], ag_recv.at[k])
        wait(arrived.at[:, span], ag_send.at[k])


def mix(inner, gathered, momentum_in, mixed, new_anchor, momentum_out):
    for t in range(gathered.shape[1]):
        rows = pl.ds(t * TILE, TILE)
        for g in range(GROUP):
            for h in range(2):
                columns = pl.ds(column_of(g, h), LANE)
                new = gathered[g, t, h]
                new_anchor[rows, columns] = new
                mixed[rows, columns] = (
                    0.5 * inner[rows, columns].astype(jnp.float32) + 0.5 * new.astype(jnp.float32)
                ).astype(jnp.bfloat16)
    momentum_out[...] = momentum_in[...]


def on_device(inner, anchor, exponent, momentum):
    rows, width = anchor.shape[1:]
    tiles = rows // TILE
    blocks = exponent.shape[-1]
    inner2 = inner.reshape(rows, width)
    chunks = len(CHUNKS)
    outside = pl.BlockSpec(memory_space=pltpu.HBM)
    inside = pl.BlockSpec(memory_space=pltpu.VMEM)
    dma = pltpu.SemaphoreType.DMA
    gathered, momentum_next = pl.pallas_call(
        exchange,
        out_shape=(
            jax.ShapeDtypeStruct((GROUP, tiles, 2, TILE, LANE), jnp.bfloat16),
            jax.ShapeDtypeStruct((rows, LANE), jnp.float32),
        ),
        in_specs=[outside] * 4,
        out_specs=(inside, inside),
        scratch_shapes=[
            pltpu.VMEM((rows, width), jnp.bfloat16),
            pltpu.VMEM((rows, width), jnp.bfloat16),
            pltpu.VMEM((blocks, rows), jnp.int32),
            pltpu.VMEM((rows, blocks), jnp.int32),
            pltpu.VMEM((blocks, width), jnp.bfloat16),
            pltpu.VMEM((rows, width), jnp.float32),
            pltpu.VMEM((rows, width), jnp.float32),
            pltpu.VMEM((GROUP, tiles, 2, TILE, LANE), jnp.bfloat16),
            pltpu.VMEM((len(PEERS), tiles, 2, TILE, LANE), jnp.bfloat16),
            pltpu.VMEM((rows, LANE), jnp.float32),
            pltpu.VMEM((tiles, 2, TILE, LANE), jnp.bfloat16),
            pltpu.VMEM((tiles, 2, TILE, LANE), jnp.bfloat16),
            dma((chunks, 2)),
            dma((2,)),
            dma((chunks,)),
            dma((chunks,)),
            dma((chunks,)),
            dma((chunks,)),
            dma((chunks,)),
            dma((chunks,)),
            pltpu.VMEM((rows, LANE), jnp.float32),
            pltpu.SemaphoreType.REGULAR,
            pltpu.SemaphoreType.REGULAR,
        ],
        compiler_params=pltpu.CompilerParams(
            collective_id=0, has_side_effects=True, vmem_limit_bytes=24 << 20
        ),
        name="exchange",
    )(
        *(
            pltpu.with_memory_space_constraint(array, pltpu.HBM)
            for array in (
                inner2,
                anchor.reshape(rows, width),
                exponent.reshape(rows, blocks).T,
                momentum.reshape(rows, LANE),
            )
        )
    )

    steps = 4
    part = rows // steps
    wide = pl.BlockSpec((part, width), lambda i: (i, 0))
    narrow = pl.BlockSpec((part, LANE), lambda i: (i, 0))
    mixed, new_anchor, momentum_next = pl.pallas_call(
        mix,
        out_shape=(
            jax.ShapeDtypeStruct((rows, width), jnp.bfloat16),
            jax.ShapeDtypeStruct((rows, width), jnp.bfloat16),
            jax.ShapeDtypeStruct((rows, LANE), jnp.float32),
        ),
        grid=(steps,),
        in_specs=[
            wide,
            pl.BlockSpec((GROUP, part // TILE, 2, TILE, LANE), lambda i: (0, i, 0, 0, 0)),
            narrow,
        ],
        out_specs=(wide, wide, narrow),
        compiler_params=pltpu.CompilerParams(vmem_limit_bytes=16 << 20),
        name="mix",
    )(inner2, gathered, momentum_next)
    return (
        mixed.reshape(inner.shape),
        new_anchor.reshape(anchor.shape),
        momentum_next.reshape(momentum.shape),
    )


def solution(mesh):
    return jax.shard_map(
        on_device,
        mesh=mesh,
        in_specs=(
            P("rep", None, "fsdp", None),
            P(None, "fsdp", None),
            P("rep", None, "fsdp", None),
            P(None, "fsdp", "rep"),
        ),
        out_specs=(P("rep", None, "fsdp", None), P(None, "fsdp", None), P(None, "fsdp", "rep")),
        check_vma=False,
    )
```

```python
import functools

import jax
import jax.numpy as jnp
from jax import lax
from jax.experimental import pallas as pl
from jax.experimental.pallas import tpu as pltpu
from jax.sharding import PartitionSpec as P

MESH = pl.DeviceIdType.MESH
BLOCK = 32
LANE = 128
TILE = 16
XS = 4
REPS = 16
MINE, OTHER = 0.5, 0.7 * 1.9 / REPS
BOUNDS = ((0.25, 0.5), (0.75, 1.0), (1.25, 1.5), (1.75, 2.0), (2.5, 3.0), (3.5, 4.0), (5.0, 6.0))
CHUNKS = (4, 4, 4, 4)
PLACES = tuple((c, x, h) for c in range(2) for x in range(XS) for h in range(2))
HEARD = 2 * XS - 1


def column_of(core, x, half):
    return (x * 4 + half * 2 + core) * LANE


SPANS = tuple((k, sum(CHUNKS[:k]), tiles) for k, tiles in enumerate(CHUNKS))


def exchange(
    inner,
    anchor,
    exponent,
    momentum,
    gathered,
    momentum_next,
    inner_v,
    anchor_v,
    exponent_v,
    power_rows,
    spread,
    scale_v,
    inverse_v,
    coded,
    pair_in,
    pairs,
    arrived,
    own_sum,
    z_out,
    z_in,
    load_sem,
    small_sem,
    core_send,
    core_recv,
    rs_send,
    rs_recv,
    z_send,
    z_recv,
    ag_send,
    ag_recv,
    out_send,
    out_recv,
    momentum_v,
    near_sem,
    far_sem,
):
    rep, fsdp = lax.axis_index("rep"), lax.axis_index("fsdp")
    x, half, core = rep // 4, (rep // 2) % 2, rep % 2
    own_column = pl.multiple_of(rep * LANE, LANE)
    other_column = pl.multiple_of((x * 4 + (1 - half) * 2 + core) * LANE, LANE)

    def beside(dx):
        there = lax.rem(x + dx, XS)
        return there, (there * 4 + half * 2 + core, fsdp)

    across = (x * 4 + (1 - half) * 2 + core, fsdp)

    partner = (x * 4 + half * 2 + 1 - core, fsdp)

    barrier = pltpu.get_barrier_semaphore()
    for dx in range(1, 4):
        hub = (lax.rem(x + dx, 4) * 4 + half * 2, fsdp)
        pl.semaphore_signal(barrier, inc=1, device_id=hub, device_id_type=MESH)

    @pl.when(core == 1)
    def _():
        pl.semaphore_signal(barrier, inc=1, device_id=partner, device_id_type=MESH)

    far = (x * 4 + (1 - half) * 2 + 1, fsdp)
    pl.semaphore_signal(barrier, inc=1, device_id=far, device_id_type=MESH)

    small = [
        pltpu.make_async_copy(exponent, exponent_v, small_sem.at[0]),
        pltpu.make_async_copy(momentum, momentum_v, small_sem.at[1]),
    ]
    small[0].start()
    loads = []
    for k, first, tiles in SPANS:
        rows = pl.ds(first * TILE, tiles * TILE)
        pair = (
            pltpu.make_async_copy(inner.at[rows], inner_v.at[rows], load_sem.at[k, 0]),
            pltpu.make_async_copy(anchor.at[rows], anchor_v.at[rows], load_sem.at[k, 1]),
        )
        for copy in pair:
            copy.start()
        loads.append(pair)
    small[1].start()

    width = anchor.shape[1]
    blocks = width // BLOCK
    block_of = lax.broadcasted_iota(jnp.int32, (blocks, width), 1) // BLOCK
    row_of = lax.broadcasted_iota(jnp.int32, (blocks, width), 0)
    spread[...] = jnp.where(block_of == row_of, 1.0, 0.0).astype(jnp.bfloat16)
    small[0].wait()
    power_rows[...] = exponent_v[...].T

    def start(source, destination, send, recv, device):
        pltpu.make_async_remote_copy(
            src_ref=source,
            dst_ref=destination,
            send_sem=send,
            recv_sem=recv,
            device_id=device,
            device_id_type=MESH,
        ).start()

    def wait(buffer, semaphore):
        pltpu.make_async_copy(buffer, buffer, semaphore).wait()

    def pass_pairs(k):
        _, first, tiles = SPANS[k]
        span = pl.ds(first, tiles)
        wait(pair_in.at[:, span], core_recv.at[k])

        def add(tile, carry):
            for place in range(XS):
                for h in range(2):
                    pairs[place, tile, h] = (
                        coded[core, place, tile, h].astype(jnp.float32)
                        + pair_in[place, tile, h].astype(jnp.float32)
                    ).astype(jnp.bfloat16)
            return carry

        lax.fori_loop(first, first + tiles, add, 0)
        for slot in range(XS - 1):
            there, device = beside(slot + 1)
            start(pairs.at[there, span], arrived.at[slot, span], rs_send.at[k], rs_recv.at[k], device)

    for k, first, tiles in SPANS:
        rows = pl.ds(first * TILE, tiles * TILE)
        powers = power_rows[rows, :]
        scale, inverse = jnp.zeros(powers.shape, jnp.float32), jnp.zeros(powers.shape, jnp.float32)
        for power in (-1, 0, 1):
            scale = jnp.where(powers == power, jnp.float32(2.0**power), scale)
            inverse = jnp.where(powers == power, jnp.float32(2.0**-power), inverse)
        for value, target in ((scale, scale_v), (inverse, inverse_v)):
            target[rows, :] = jnp.dot(
                value.astype(jnp.bfloat16), spread[...], preferred_element_type=jnp.float32
            )
        for copy in loads[k]:
            copy.wait()

        def code(tile, carry):
            rows = pl.ds(pl.multiple_of(tile * TILE, TILE), TILE)
            for c, place, h in PLACES:
                columns = pl.ds(column_of(c, place, h), LANE)
                delta = anchor_v[rows, columns].astype(jnp.float32) - inner_v[
                    rows, columns
                ].astype(jnp.float32)
                magnitude = jnp.abs(delta) * inverse_v[rows, columns]
                scale = scale_v[rows, columns]
                level = jnp.zeros(delta.shape, jnp.float32)
                for bound, height in BOUNDS:
                    level = jnp.where(magnitude >= bound, jnp.float32(height), level)
                level = level * jnp.where(delta < 0, -scale, scale)
                coded[c, place, tile, h] = level.astype(jnp.bfloat16)
            return carry

        lax.fori_loop(first, first + tiles, code, 0)

        if k == 0:

            @pl.when(core == 0)
            def _():
                pl.semaphore_wait(barrier, HEARD)
                pl.semaphore_signal(near_sem, inc=1, device_id=partner, device_id_type=MESH)

            @pl.when(core == 1)
            def _():
                pl.semaphore_wait(near_sem, 1)

        span = pl.ds(first, tiles)
        start(
            coded.at[1 - core, :, span], pair_in.at[:, span], core_send.at[k], core_recv.at[k], partner
        )
        if k > 0:
            pass_pairs(k - 1)
    pass_pairs(len(CHUNKS) - 1)

    @pl.when(core == 1)
    def _():
        pl.semaphore_wait(barrier, 2)
        pl.semaphore_signal(far_sem, inc=1, device_id=partner, device_id_type=MESH)

    @pl.when(core == 0)
    def _():
        pl.semaphore_wait(far_sem, 1)

    small[1].wait()
    for k, first, tiles in SPANS:
        span = pl.ds(first, tiles)
        wait(arrived.at[:, span], rs_recv.at[k])

        def add(tile, carry):
            rows = pl.ds(pl.multiple_of(tile * TILE, TILE), TILE)
            own = pairs[x, tile, half].astype(jnp.float32)
            other = pairs[x, tile, 1 - half].astype(jnp.float32)
            for slot in range(XS - 1):
                own = own + arrived[slot, tile, half].astype(jnp.float32)
                other = other + arrived[slot, tile, 1 - half].astype(jnp.float32)
            anchor_own = anchor_v[rows, pl.ds(own_column, LANE)].astype(jnp.float32)
            mine = MINE * anchor_own - OTHER * own - (0.7 * 0.81) * momentum_v[rows, :]
            own_sum[rows, :] = own
            z_out[tile, 0] = mine.astype(jnp.bfloat16)
            z_out[tile, 1] = other.astype(jnp.bfloat16)
            return carry

        lax.fori_loop(first, first + tiles, add, 0)
        start(z_out.at[span], z_in.at[span], z_send.at[k], z_recv.at[k], across)

    def hand_over(k):
        _, first, tiles = SPANS[k]
        span = pl.ds(first, tiles)
        wait(arrived.at[:, span], ag_recv.at[k])
        whole = gathered.at[core, :, span]
        start(whole, whole, out_send.at[k], out_recv.at[k], partner)

    for k, first, tiles in SPANS:
        span = pl.ds(first, tiles)
        wait(z_in.at[span], z_recv.at[k])

        def update(tile, carry):
            rows = pl.ds(pl.multiple_of(tile * TILE, TILE), TILE)

            def new(column, part, sums):
                wide = anchor_v[rows, pl.ds(column, LANE)].astype(jnp.float32)
                rest = (1.0 - MINE) * wide - OTHER * sums.astype(jnp.float32)
                return (part.astype(jnp.float32) + rest).astype(jnp.bfloat16)

            theirs = z_in[tile, 1]
            gathered[core, x, tile, half] = new(own_column, z_out[tile, 0], theirs)
            gathered[core, x, tile, 1 - half] = new(other_column, z_in[tile, 0], z_out[tile, 1])
            outer_grad = (own_sum[rows, :] + theirs.astype(jnp.float32)) * (1.0 / REPS)
            momentum_next[rows, :] = 0.9 * momentum_v[rows, :] + outer_grad
            return carry

        lax.fori_loop(first, first + tiles, update, 0)
        piece = gathered.at[core, x, span]
        for slot in range(XS - 1):
            start(piece, piece, ag_send.at[k], ag_recv.at[k], beside(slot + 1)[1])
        if k > 0:
            hand_over(k - 1)
    hand_over(len(CHUNKS) - 1)

    for k, first, tiles in SPANS:
        span = pl.ds(first, tiles)
        wait(pair_in.at[:, span], core_send.at[k])
        wait(arrived.at[:, span], rs_send.at[k])
        wait(z_out.at[span], z_send.at[k])
        wait(arrived.at[:, span], ag_send.at[k])
        wait(pair_in.at[:, span], out_send.at[k])
    for k, first, tiles in SPANS:
        wait(pair_in.at[:, pl.ds(first, tiles)], out_recv.at[k])


def mix(inner, gathered, momentum_in, mixed, new_anchor, momentum_out):
    for t in range(gathered.shape[2]):
        rows = pl.ds(t * TILE, TILE)
        for c, x, h in PLACES:
            columns = pl.ds(column_of(c, x, h), LANE)
            new = gathered[c, x, t, h]
            new_anchor[rows, columns] = new
            mixed[rows, columns] = (
                0.5 * inner[rows, columns].astype(jnp.float32) + 0.5 * new.astype(jnp.float32)
            ).astype(jnp.bfloat16)
    momentum_out[...] = momentum_in[...]


def on_device(inner, anchor, exponent, momentum):
    rows, width = anchor.shape[1:]
    tiles = rows // TILE
    blocks = exponent.shape[-1]
    inner2 = inner.reshape(rows, width)
    chunks = len(CHUNKS)
    outside = pl.BlockSpec(memory_space=pltpu.HBM)
    inside = pl.BlockSpec(memory_space=pltpu.VMEM)
    dma = pltpu.SemaphoreType.DMA
    gathered, momentum_next = pl.pallas_call(
        exchange,
        out_shape=(
            jax.ShapeDtypeStruct((2, XS, tiles, 2, TILE, LANE), jnp.bfloat16),
            jax.ShapeDtypeStruct((rows, LANE), jnp.float32),
        ),
        in_specs=[outside] * 4,
        out_specs=(inside, inside),
        scratch_shapes=[
            pltpu.VMEM((rows, width), jnp.bfloat16),
            pltpu.VMEM((rows, width), jnp.bfloat16),
            pltpu.VMEM((blocks, rows), jnp.int32),
            pltpu.VMEM((rows, blocks), jnp.int32),
            pltpu.VMEM((blocks, width), jnp.bfloat16),
            pltpu.VMEM((rows, width), jnp.float32),
            pltpu.VMEM((rows, width), jnp.float32),
            pltpu.VMEM((2, XS, tiles, 2, TILE, LANE), jnp.bfloat16),
            pltpu.VMEM((XS, tiles, 2, TILE, LANE), jnp.bfloat16),
            pltpu.VMEM((XS, tiles, 2, TILE, LANE), jnp.bfloat16),
            pltpu.VMEM((XS - 1, tiles, 2, TILE, LANE), jnp.bfloat16),
            pltpu.VMEM((rows, LANE), jnp.float32),
            pltpu.VMEM((tiles, 2, TILE, LANE), jnp.bfloat16),
            pltpu.VMEM((tiles, 2, TILE, LANE), jnp.bfloat16),
            dma((chunks, 2)),
            dma((2,)),
            *[dma((chunks,))] * 10,
            pltpu.VMEM((rows, LANE), jnp.float32),
            pltpu.SemaphoreType.REGULAR,
            pltpu.SemaphoreType.REGULAR,
        ],
        compiler_params=pltpu.CompilerParams(
            collective_id=0, has_side_effects=True, vmem_limit_bytes=24 << 20
        ),
        name="exchange",
    )(
        *(
            pltpu.with_memory_space_constraint(array, pltpu.HBM)
            for array in (
                inner2,
                anchor.reshape(rows, width),
                exponent.reshape(rows, blocks).T,
                momentum.reshape(rows, LANE),
            )
        )
    )

    steps = 4
    part = rows // steps
    wide = pl.BlockSpec((part, width), lambda i: (i, 0))
    narrow = pl.BlockSpec((part, LANE), lambda i: (i, 0))
    mixed, new_anchor, momentum_next = pl.pallas_call(
        mix,
        out_shape=(
            jax.ShapeDtypeStruct((rows, width), jnp.bfloat16),
            jax.ShapeDtypeStruct((rows, width), jnp.bfloat16),
            jax.ShapeDtypeStruct((rows, LANE), jnp.float32),
        ),
        grid=(steps,),
        in_specs=[
            wide,
            pl.BlockSpec((2, XS, part // TILE, 2, TILE, LANE), lambda i: (0, 0, i, 0, 0, 0)),
            narrow,
        ],
        out_specs=(wide, wide, narrow),
        compiler_params=pltpu.CompilerParams(vmem_limit_bytes=16 << 20),
        name="mix",
    )(inner2, gathered, momentum_next)
    return (
        mixed.reshape(inner.shape),
        new_anchor.reshape(anchor.shape),
        momentum_next.reshape(momentum.shape),
    )


def solution(mesh):
    return jax.shard_map(
        on_device,
        mesh=mesh,
        in_specs=(
            P("rep", None, "fsdp", None),
            P(None, "fsdp", None),
            P("rep", None, "fsdp", None),
            P(None, "fsdp", "rep"),
        ),
        out_specs=(P("rep", None, "fsdp", None), P(None, "fsdp", None), P(None, "fsdp", "rep")),
        check_vma=False,
    )
```

```python
import functools

import jax
import jax.numpy as jnp
from jax import lax
from jax.experimental import pallas as pl
from jax.experimental.pallas import tpu as pltpu
from jax.sharding import PartitionSpec as P

MESH = pl.DeviceIdType.MESH
BLOCK = 32
LANE = 128
TILE = 16
XS = 4
REPS = 16
MINE, OTHER = 0.5, 0.7 * 1.9 / REPS
BOUNDS = ((0.25, 0.5), (0.75, 1.0), (1.25, 1.5), (1.75, 2.0), (2.5, 3.0), (3.5, 4.0), (5.0, 6.0))
CHUNKS = (1, 2, 3, 4, 3, 2, 1)
HOPS = len(CHUNKS) - 2
PLACES = tuple((c, x, h) for c in range(2) for x in range(XS) for h in range(2))
HEARD = 2 * XS - 1


def column_of(core, x, half):
    return (x * 4 + half * 2 + core) * LANE


AHEAD = 2
SPANS = tuple((k, sum(CHUNKS[:k]), tiles) for k, tiles in enumerate(CHUNKS))


def exchange(
    inner,
    anchor,
    exponent,
    momentum,
    mixed,
    new_anchor,
    momentum_next,
    gathered,
    inner_v,
    anchor_v,
    exponent_v,
    power_rows,
    spread,
    scale_v,
    inverse_v,
    coded,
    pair_in,
    pairs,
    arrived,
    own_sum,
    z_out,
    z_in,
    load_sem,
    small_sem,
    core_send,
    core_recv,
    rs_send,
    rs_recv,
    z_send,
    z_recv,
    ag_send,
    ag_recv,
    out_send,
    out_recv,
    momentum_v,
    near_sem,
    far_sem,
):
    rep, fsdp = lax.axis_index("rep"), lax.axis_index("fsdp")
    x, half, core = rep // 4, (rep // 2) % 2, rep % 2
    own_column = pl.multiple_of(rep * LANE, LANE)
    other_column = pl.multiple_of((x * 4 + (1 - half) * 2 + core) * LANE, LANE)

    def beside(dx, there_core):
        there = lax.rem(x + dx, XS)
        return there, (there * 4 + half * 2 + there_core, fsdp)

    across = (x * 4 + (1 - half) * 2 + core, fsdp)

    partner = (x * 4 + half * 2 + 1 - core, fsdp)

    barrier = pltpu.get_barrier_semaphore()
    for dx in range(1, 4):
        hub = (lax.rem(x + dx, 4) * 4 + half * 2, fsdp)
        pl.semaphore_signal(barrier, inc=1, device_id=hub, device_id_type=MESH)

    @pl.when(core == 1)
    def _():
        pl.semaphore_signal(barrier, inc=1, device_id=partner, device_id_type=MESH)

    far = (x * 4 + (1 - half) * 2 + 1, fsdp)
    pl.semaphore_signal(barrier, inc=1, device_id=far, device_id_type=MESH)

    small = [
        pltpu.make_async_copy(exponent, exponent_v, small_sem.at[0]),
        pltpu.make_async_copy(momentum, momentum_v, small_sem.at[1]),
    ]
    small[0].start()
    loads = []
    for k, first, tiles in SPANS:
        rows = pl.ds(first * TILE, tiles * TILE)
        pair = (
            pltpu.make_async_copy(inner.at[rows], inner_v.at[rows], load_sem.at[k, 0]),
            pltpu.make_async_copy(anchor.at[rows], anchor_v.at[rows], load_sem.at[k, 1]),
        )
        for copy in pair:
            copy.start()
        loads.append(pair)
    small[1].start()

    width = anchor.shape[1]
    blocks = width // BLOCK
    block_of = lax.broadcasted_iota(jnp.int32, (blocks, width), 1) // BLOCK
    row_of = lax.broadcasted_iota(jnp.int32, (blocks, width), 0)
    spread[...] = jnp.where(block_of == row_of, 1.0, 0.0).astype(jnp.bfloat16)
    small[0].wait()
    power_rows[...] = exponent_v[...].T

    def start(source, destination, send, recv, device):
        pltpu.make_async_remote_copy(
            src_ref=source,
            dst_ref=destination,
            send_sem=send,
            recv_sem=recv,
            device_id=device,
            device_id_type=MESH,
        ).start()

    def wait(buffer, semaphore):
        pltpu.make_async_copy(buffer, buffer, semaphore).wait()

    def pass_pairs(k):
        _, first, tiles = SPANS[k]
        span = pl.ds(first, tiles)
        wait(pair_in.at[:, span], core_recv.at[k])

        def add(tile, carry):
            for place in range(XS):
                for h in range(2):
                    pairs[place, tile, h] = (
                        coded[core, place, tile, h].astype(jnp.float32)
                        + pair_in[place, tile, h].astype(jnp.float32)
                    ).astype(jnp.bfloat16)
            return carry

        lax.fori_loop(first, first + tiles, add, 0)
        for slot in (1, 0, 2):
            there, device = beside(slot + 1, core)
            start(pairs.at[there, span], arrived.at[slot, span], rs_send.at[k], rs_recv.at[k], device)

    for k, first, tiles in SPANS:
        rows = pl.ds(first * TILE, tiles * TILE)
        powers = power_rows[rows, :]
        scale, inverse = jnp.zeros(powers.shape, jnp.float32), jnp.zeros(powers.shape, jnp.float32)
        for power in (-1, 0, 1):
            scale = jnp.where(powers == power, jnp.float32(2.0**power), scale)
            inverse = jnp.where(powers == power, jnp.float32(2.0**-power), inverse)
        for value, target in ((scale, scale_v), (inverse, inverse_v)):
            target[rows, :] = jnp.dot(
                value.astype(jnp.bfloat16), spread[...], preferred_element_type=jnp.float32
            )
        for copy in loads[k]:
            copy.wait()

        def code(tile, carry):
            rows = pl.ds(pl.multiple_of(tile * TILE, TILE), TILE)
            for c, place, h in PLACES:
                columns = pl.ds(column_of(c, place, h), LANE)
                delta = anchor_v[rows, columns].astype(jnp.float32) - inner_v[
                    rows, columns
                ].astype(jnp.float32)
                magnitude = jnp.abs(delta) * inverse_v[rows, columns]
                scale = scale_v[rows, columns]
                level = jnp.zeros(delta.shape, jnp.float32)
                for bound, height in BOUNDS:
                    level = jnp.where(magnitude >= bound, jnp.float32(height), level)
                level = level * jnp.where(delta < 0, -scale, scale)
                coded[c, place, tile, h] = level.astype(jnp.bfloat16)
            return carry

        lax.fori_loop(first, first + tiles, code, 0)

        if k == 0:

            @pl.when(core == 0)
            def _():
                pl.semaphore_wait(barrier, HEARD)
                pl.semaphore_signal(near_sem, inc=1, device_id=partner, device_id_type=MESH)

            @pl.when(core == 1)
            def _():
                pl.semaphore_wait(near_sem, 1)

        span = pl.ds(first, tiles)
        start(
            coded.at[1 - core, :, span], pair_in.at[:, span], core_send.at[k], core_recv.at[k], partner
        )
        if k >= AHEAD:
            pass_pairs(k - AHEAD)
    for k in range(len(CHUNKS) - AHEAD, len(CHUNKS)):
        pass_pairs(k)

    @pl.when(core == 1)
    def _():
        pl.semaphore_wait(barrier, 2)
        pl.semaphore_signal(far_sem, inc=1, device_id=partner, device_id_type=MESH)

    @pl.when(core == 0)
    def _():
        pl.semaphore_wait(far_sem, 1)

    small[1].wait()
    for k, first, tiles in SPANS:
        span = pl.ds(first, tiles)
        wait(arrived.at[:, span], rs_recv.at[k])

        def add(tile, carry):
            rows = pl.ds(pl.multiple_of(tile * TILE, TILE), TILE)
            own = pairs[x, tile, half].astype(jnp.float32)
            other = pairs[x, tile, 1 - half].astype(jnp.float32)
            for slot in range(XS - 1):
                own = own + arrived[slot, tile, half].astype(jnp.float32)
                other = other + arrived[slot, tile, 1 - half].astype(jnp.float32)
            anchor_own = anchor_v[rows, pl.ds(own_column, LANE)].astype(jnp.float32)
            mine = MINE * anchor_own - OTHER * own - (0.7 * 0.81) * momentum_v[rows, :]
            own_sum[rows, :] = own
            z_out[tile, 0] = mine.astype(jnp.bfloat16)
            z_out[tile, 1] = other.astype(jnp.bfloat16)
            return carry

        lax.fori_loop(first, first + tiles, add, 0)
        start(z_out.at[span], z_in.at[span], z_send.at[k], z_recv.at[k], across)

    def hand_over(k):
        _, first, tiles = SPANS[k]
        span = pl.ds(first, tiles)
        wait(arrived.at[:, span], ag_recv.at[k])
        whole = gathered.at[core, :, span]
        start(whole, whole, out_send.at[k], out_recv.at[k], partner)

    def mix(k):
        _, first, tiles = SPANS[k]
        span = pl.ds(first, tiles)
        if k >= HOPS:
            wait(arrived.at[:, span], ag_recv.at[k])
        wait(pair_in.at[:, span], out_recv.at[k])

        def part(tile, carry):
            rows = pl.ds(pl.multiple_of(tile * TILE, TILE), TILE)
            for c, place, h in PLACES:
                columns = pl.ds(column_of(c, place, h), LANE)
                new = gathered[c, place, tile, h]
                new_anchor[rows, columns] = new
                mixed[rows, columns] = (
                    0.5 * inner_v[rows, columns].astype(jnp.float32)
                    + 0.5 * new.astype(jnp.float32)
                ).astype(jnp.bfloat16)
            return carry

        lax.fori_loop(first, first + tiles, part, 0)

    for k, first, tiles in SPANS:
        span = pl.ds(first, tiles)
        wait(z_in.at[span], z_recv.at[k])

        def update(tile, carry):
            rows = pl.ds(pl.multiple_of(tile * TILE, TILE), TILE)

            def new(column, part, sums):
                wide = anchor_v[rows, pl.ds(column, LANE)].astype(jnp.float32)
                rest = (1.0 - MINE) * wide - OTHER * sums.astype(jnp.float32)
                return (part.astype(jnp.float32) + rest).astype(jnp.bfloat16)

            theirs = z_in[tile, 1]
            gathered[core, x, tile, half] = new(own_column, z_out[tile, 0], theirs)
            gathered[core, x, tile, 1 - half] = new(other_column, z_in[tile, 0], z_out[tile, 1])
            outer_grad = (own_sum[rows, :] + theirs.astype(jnp.float32)) * (1.0 / REPS)
            momentum_next[rows, :] = 0.9 * momentum_v[rows, :] + outer_grad
            return carry

        lax.fori_loop(first, first + tiles, update, 0)
        piece = gathered.at[core, x, span]
        for slot in (1, 0, 2):
            start(piece, piece, ag_send.at[k], ag_recv.at[k], beside(slot + 1, core)[1])
        if k >= HOPS:
            for slot in (1, 0, 2):
                other_core = beside(slot + 1, 1 - core)[1]
                start(piece, piece, out_send.at[k], out_recv.at[k], other_core)
            start(piece, piece, out_send.at[k], out_recv.at[k], partner)
        elif k > 0:
            hand_over(k - 1)
        if 2 <= k <= HOPS:
            mix(k - 2)
    hand_over(HOPS - 1)
    for k in range(HOPS - 1, len(CHUNKS)):
        mix(k)

    for k, first, tiles in SPANS:
        span = pl.ds(first, tiles)
        wait(pair_in.at[:, span], core_send.at[k])
        wait(arrived.at[:, span], rs_send.at[k])
        wait(z_out.at[span], z_send.at[k])
        wait(arrived.at[:, span], ag_send.at[k])
        wait(pair_in.at[:, span], out_send.at[k])


def flush(*refs):
    results, outputs, sems = refs[:3], refs[3:6], refs[6]
    copies = [
        pltpu.make_async_copy(result, output, sems.at[i])
        for i, (result, output) in enumerate(zip(results, outputs))
    ]
    for copy in copies:
        copy.start()
    for copy in copies:
        copy.wait()


def on_device(inner, anchor, exponent, momentum):
    rows, width = anchor.shape[1:]
    tiles = rows // TILE
    blocks = exponent.shape[-1]
    inner2 = inner.reshape(rows, width)
    chunks = len(CHUNKS)
    outside = pl.BlockSpec(memory_space=pltpu.HBM)
    inside = pl.BlockSpec(memory_space=pltpu.VMEM)
    dma = pltpu.SemaphoreType.DMA
    results = (
        jax.ShapeDtypeStruct((rows, width), jnp.bfloat16),
        jax.ShapeDtypeStruct((rows, width), jnp.bfloat16),
        jax.ShapeDtypeStruct((rows, LANE), jnp.float32),
    )
    inside_results = pl.pallas_call(
        exchange,
        out_shape=results,
        in_specs=[outside] * 4,
        out_specs=(inside,) * 3,
        scratch_shapes=[
            pltpu.VMEM((2, XS, tiles, 2, TILE, LANE), jnp.bfloat16),
            pltpu.VMEM((rows, width), jnp.bfloat16),
            pltpu.VMEM((rows, width), jnp.bfloat16),
            pltpu.VMEM((blocks, rows), jnp.int32),
            pltpu.VMEM((rows, blocks), jnp.int32),
            pltpu.VMEM((blocks, width), jnp.bfloat16),
            pltpu.VMEM((rows, width), jnp.float32),
            pltpu.VMEM((rows, width), jnp.float32),
            pltpu.VMEM((2, XS, tiles, 2, TILE, LANE), jnp.bfloat16),
            pltpu.VMEM((XS, tiles, 2, TILE, LANE), jnp.bfloat16),
            pltpu.VMEM((XS, tiles, 2, TILE, LANE), jnp.bfloat16),
            pltpu.VMEM((XS - 1, tiles, 2, TILE, LANE), jnp.bfloat16),
            pltpu.VMEM((rows, LANE), jnp.float32),
            pltpu.VMEM((tiles, 2, TILE, LANE), jnp.bfloat16),
            pltpu.VMEM((tiles, 2, TILE, LANE), jnp.bfloat16),
            dma((chunks, 2)),
            dma((2,)),
            *[dma((chunks,))] * 10,
            pltpu.VMEM((rows, LANE), jnp.float32),
            pltpu.SemaphoreType.REGULAR,
            pltpu.SemaphoreType.REGULAR,
        ],
        compiler_params=pltpu.CompilerParams(
            collective_id=0, has_side_effects=True, vmem_limit_bytes=24 << 20
        ),
        name="exchange",
    )(
        *(
            pltpu.with_memory_space_constraint(array, pltpu.HBM)
            for array in (
                inner2,
                anchor.reshape(rows, width),
                exponent.reshape(rows, blocks).T,
                momentum.reshape(rows, LANE),
            )
        )
    )

    anywhere = pl.BlockSpec(memory_space=pl.ANY)
    mixed, new_anchor, momentum_next = pl.pallas_call(
        flush,
        out_shape=results,
        in_specs=[anywhere] * 3,
        out_specs=(anywhere,) * 3,
        scratch_shapes=[dma((3,))],
        compiler_params=pltpu.CompilerParams(vmem_limit_bytes=16 << 20),
        name="flush",
    )(*inside_results)
    return (
        mixed.reshape(inner.shape),
        new_anchor.reshape(anchor.shape),
        momentum_next.reshape(momentum.shape),
    )


def solution(mesh):
    return jax.shard_map(
        on_device,
        mesh=mesh,
        in_specs=(
            P("rep", None, "fsdp", None),
            P(None, "fsdp", None),
            P("rep", None, "fsdp", None),
            P(None, "fsdp", "rep"),
        ),
        out_specs=(P("rep", None, "fsdp", None), P(None, "fsdp", None), P(None, "fsdp", "rep")),
        check_vma=False,
    )
```

```python
import functools

import jax
import jax.numpy as jnp
from jax import lax
from jax.experimental import pallas as pl
from jax.experimental.pallas import tpu as pltpu
from jax.sharding import PartitionSpec as P

MESH = pl.DeviceIdType.MESH
BLOCK = 32
LANE = 128
TILE = 16
XS = 4
REPS = 16
MINE, OTHER = 0.5, 0.7 * 1.9 / REPS
BOUNDS = ((0.25, 0.5), (0.75, 1.0), (1.25, 1.5), (1.75, 2.0), (2.5, 3.0), (3.5, 4.0), (5.0, 6.0))
CHUNKS = (1, 2, 3, 4, 3, 2, 1)
HOPS = len(CHUNKS) - 2
PLACES = tuple((c, x, h) for c in range(2) for x in range(XS) for h in range(2))
HEARD = 2 * XS - 1


def column_of(core, x, half):
    return (x * 4 + half * 2 + core) * LANE


AHEAD = 2
SPANS = tuple((k, sum(CHUNKS[:k]), tiles) for k, tiles in enumerate(CHUNKS))


def exchange(
    inner,
    anchor,
    exponent,
    momentum,
    mixed,
    new_anchor,
    momentum_next,
    gathered,
    inner_v,
    anchor_v,
    exponent_v,
    power_rows,
    spread,
    scale_v,
    inverse_v,
    coded,
    pair_in,
    pairs,
    arrived,
    own_sum,
    z_out,
    z_in,
    load_sem,
    small_sem,
    core_send,
    core_recv,
    rs_send,
    rs_recv,
    z_send,
    z_recv,
    ag_send,
    ag_recv,
    out_send,
    out_recv,
    momentum_v,
    near_sem,
    far_sem,
):
    rep, fsdp = lax.axis_index("rep"), lax.axis_index("fsdp")
    x, half, core = rep // 4, (rep // 2) % 2, rep % 2
    own_column = pl.multiple_of(rep * LANE, LANE)
    other_column = pl.multiple_of((x * 4 + (1 - half) * 2 + core) * LANE, LANE)

    def beside(dx, there_core):
        there = lax.rem(x + dx, XS)
        return there, (there * 4 + half * 2 + there_core, fsdp)

    across = (x * 4 + (1 - half) * 2 + core, fsdp)

    partner = (x * 4 + half * 2 + 1 - core, fsdp)

    barrier = pltpu.get_barrier_semaphore()
    for dx in range(1, 4):
        hub = (lax.rem(x + dx, 4) * 4 + half * 2, fsdp)
        pl.semaphore_signal(barrier, inc=1, device_id=hub, device_id_type=MESH)

    @pl.when(core == 1)
    def _():
        pl.semaphore_signal(barrier, inc=1, device_id=partner, device_id_type=MESH)

    far = (x * 4 + (1 - half) * 2 + 1, fsdp)
    pl.semaphore_signal(barrier, inc=1, device_id=far, device_id_type=MESH)

    small = [
        pltpu.make_async_copy(exponent, exponent_v, small_sem.at[0]),
        pltpu.make_async_copy(momentum, momentum_v, small_sem.at[1]),
    ]
    small[0].start()
    loads = []
    for k, first, tiles in SPANS:
        rows = pl.ds(first * TILE, tiles * TILE)
        pair = (
            pltpu.make_async_copy(inner.at[rows], inner_v.at[rows], load_sem.at[k, 0]),
            pltpu.make_async_copy(anchor.at[rows], anchor_v.at[rows], load_sem.at[k, 1]),
        )
        for copy in pair:
            copy.start()
        loads.append(pair)
    small[1].start()

    width = anchor.shape[1]
    blocks = width // BLOCK
    block_of = lax.broadcasted_iota(jnp.int32, (blocks, width), 1) // BLOCK
    row_of = lax.broadcasted_iota(jnp.int32, (blocks, width), 0)
    spread[...] = jnp.where(block_of == row_of, 1.0, 0.0).astype(jnp.bfloat16)
    small[0].wait()
    power_rows[...] = exponent_v[...].T

    def start(source, destination, send, recv, device):
        pltpu.make_async_remote_copy(
            src_ref=source,
            dst_ref=destination,
            send_sem=send,
            recv_sem=recv,
            device_id=device,
            device_id_type=MESH,
        ).start()

    def wait(buffer, semaphore):
        pltpu.make_async_copy(buffer, buffer, semaphore).wait()

    def pass_pairs(k):
        _, first, tiles = SPANS[k]
        span = pl.ds(first, tiles)
        wait(pair_in.at[:, span], core_recv.at[k])

        def add(tile, carry):
            for place in range(XS):
                for h in range(2):
                    pairs[place, tile, h] = (
                        coded[core, place, tile, h].astype(jnp.float32)
                        + pair_in[place, tile, h].astype(jnp.float32)
                    ).astype(jnp.bfloat16)
            return carry

        lax.fori_loop(first, first + tiles, add, 0)
        for slot in (1, 0, 2):
            there, device = beside(slot + 1, core)
            start(pairs.at[there, span], arrived.at[slot, span], rs_send.at[k], rs_recv.at[k], device)

    for k, first, tiles in SPANS:
        rows = pl.ds(first * TILE, tiles * TILE)
        powers = power_rows[rows, :]
        scale, inverse = jnp.zeros(powers.shape, jnp.float32), jnp.zeros(powers.shape, jnp.float32)
        for power in (-1, 0, 1):
            scale = jnp.where(powers == power, jnp.float32(2.0**power), scale)
            inverse = jnp.where(powers == power, jnp.float32(2.0**-power), inverse)
        for value, target in ((scale, scale_v), (inverse, inverse_v)):
            target[rows, :] = jnp.dot(
                value.astype(jnp.bfloat16), spread[...], preferred_element_type=jnp.float32
            )
        for copy in loads[k]:
            copy.wait()

        def code(tile, carry):
            rows = pl.ds(pl.multiple_of(tile * TILE, TILE), TILE)
            for c, place, h in PLACES:
                columns = pl.ds(column_of(c, place, h), LANE)
                delta = anchor_v[rows, columns].astype(jnp.float32) - inner_v[
                    rows, columns
                ].astype(jnp.float32)
                magnitude = jnp.abs(delta) * inverse_v[rows, columns]
                scale = scale_v[rows, columns]
                level = jnp.zeros(delta.shape, jnp.float32)
                for bound, height in BOUNDS:
                    level = jnp.where(magnitude >= bound, jnp.float32(height), level)
                level = level * jnp.where(delta < 0, -scale, scale)
                coded[c, place, tile, h] = level.astype(jnp.bfloat16)
            return carry

        lax.fori_loop(first, first + tiles, code, 0)

        if k == 0:

            @pl.when(core == 0)
            def _():
                pl.semaphore_wait(barrier, HEARD)
                pl.semaphore_signal(near_sem, inc=1, device_id=partner, device_id_type=MESH)

            @pl.when(core == 1)
            def _():
                pl.semaphore_wait(near_sem, 1)

        span = pl.ds(first, tiles)
        start(
            coded.at[1 - core, :, span], pair_in.at[:, span], core_send.at[k], core_recv.at[k], partner
        )
        if k >= AHEAD:
            pass_pairs(k - AHEAD)
    for k in range(len(CHUNKS) - AHEAD, len(CHUNKS)):
        pass_pairs(k)

    @pl.when(core == 1)
    def _():
        pl.semaphore_wait(barrier, 2)
        pl.semaphore_signal(far_sem, inc=1, device_id=partner, device_id_type=MESH)

    @pl.when(core == 0)
    def _():
        pl.semaphore_wait(far_sem, 1)

    small[1].wait()
    for k, first, tiles in SPANS:
        span = pl.ds(first, tiles)
        wait(arrived.at[:, span], rs_recv.at[k])

        def add(tile, carry):
            rows = pl.ds(pl.multiple_of(tile * TILE, TILE), TILE)
            own = pairs[x, tile, half].astype(jnp.float32)
            other = pairs[x, tile, 1 - half].astype(jnp.float32)
            for slot in range(XS - 1):
                own = own + arrived[slot, tile, half].astype(jnp.float32)
                other = other + arrived[slot, tile, 1 - half].astype(jnp.float32)
            anchor_own = anchor_v[rows, pl.ds(own_column, LANE)].astype(jnp.float32)
            mine = MINE * anchor_own - OTHER * own - (0.7 * 0.81) * momentum_v[rows, :]
            own_sum[rows, :] = own
            z_out[tile, 0] = mine.astype(jnp.bfloat16)
            z_out[tile, 1] = other.astype(jnp.bfloat16)
            return carry

        lax.fori_loop(first, first + tiles, add, 0)

        @pl.when(half == 1)
        def _():
            wait(z_in.at[span], z_recv.at[k])

        start(z_out.at[span], z_in.at[span], z_send.at[k], z_recv.at[k], across)

    def hand_over(k):
        _, first, tiles = SPANS[k]
        span = pl.ds(first, tiles)
        wait(arrived.at[:, span], ag_recv.at[k])
        whole = gathered.at[core, :, span]
        start(whole, whole, out_send.at[k], out_recv.at[k], partner)

    def mix(k):
        _, first, tiles = SPANS[k]
        span = pl.ds(first, tiles)
        if k >= HOPS:
            wait(arrived.at[:, span], ag_recv.at[k])
        wait(pair_in.at[:, span], out_recv.at[k])

        def part(tile, carry):
            rows = pl.ds(pl.multiple_of(tile * TILE, TILE), TILE)
            for c, place, h in PLACES:
                columns = pl.ds(column_of(c, place, h), LANE)
                new = gathered[c, place, tile, h]
                new_anchor[rows, columns] = new
                mixed[rows, columns] = (
                    0.5 * inner_v[rows, columns].astype(jnp.float32)
                    + 0.5 * new.astype(jnp.float32)
                ).astype(jnp.bfloat16)
            return carry

        lax.fori_loop(first, first + tiles, part, 0)

    for k, first, tiles in SPANS:
        span = pl.ds(first, tiles)

        @pl.when(half == 0)
        def _():
            wait(z_in.at[span], z_recv.at[k])

        def update(tile, carry):
            rows = pl.ds(pl.multiple_of(tile * TILE, TILE), TILE)

            def new(column, part, sums):
                wide = anchor_v[rows, pl.ds(column, LANE)].astype(jnp.float32)
                rest = (1.0 - MINE) * wide - OTHER * sums.astype(jnp.float32)
                return (part.astype(jnp.float32) + rest).astype(jnp.bfloat16)

            theirs = z_in[tile, 1]
            gathered[core, x, tile, half] = new(own_column, z_out[tile, 0], theirs)
            gathered[core, x, tile, 1 - half] = new(other_column, z_in[tile, 0], z_out[tile, 1])
            outer_grad = (own_sum[rows, :] + theirs.astype(jnp.float32)) * (1.0 / REPS)
            momentum_next[rows, :] = 0.9 * momentum_v[rows, :] + outer_grad
            return carry

        lax.fori_loop(first, first + tiles, update, 0)
        piece = gathered.at[core, x, span]
        for slot in (1, 0, 2):
            start(piece, piece, ag_send.at[k], ag_recv.at[k], beside(slot + 1, core)[1])
        if k >= HOPS:
            for slot in (1, 0, 2):
                other_core = beside(slot + 1, 1 - core)[1]
                start(piece, piece, out_send.at[k], out_recv.at[k], other_core)
            start(piece, piece, out_send.at[k], out_recv.at[k], partner)
    for k in range(HOPS):
        hand_over(k)
    for k in range(len(CHUNKS)):
        mix(k)

    for k, first, tiles in SPANS:
        span = pl.ds(first, tiles)
        wait(pair_in.at[:, span], core_send.at[k])
        wait(arrived.at[:, span], rs_send.at[k])
        wait(z_out.at[span], z_send.at[k])
        wait(arrived.at[:, span], ag_send.at[k])
        wait(pair_in.at[:, span], out_send.at[k])


def flush(*refs):
    results, outputs, sems = refs[:3], refs[3:6], refs[6]
    copies = [
        pltpu.make_async_copy(result, output, sems.at[i])
        for i, (result, output) in enumerate(zip(results, outputs))
    ]
    for copy in copies:
        copy.start()
    for copy in copies:
        copy.wait()


def on_device(inner, anchor, exponent, momentum):
    rows, width = anchor.shape[1:]
    tiles = rows // TILE
    blocks = exponent.shape[-1]
    inner2 = inner.reshape(rows, width)
    chunks = len(CHUNKS)
    outside = pl.BlockSpec(memory_space=pltpu.HBM)
    inside = pl.BlockSpec(memory_space=pltpu.VMEM)
    dma = pltpu.SemaphoreType.DMA
    results = (
        jax.ShapeDtypeStruct((rows, width), jnp.bfloat16),
        jax.ShapeDtypeStruct((rows, width), jnp.bfloat16),
        jax.ShapeDtypeStruct((rows, LANE), jnp.float32),
    )
    inside_results = pl.pallas_call(
        exchange,
        out_shape=results,
        in_specs=[outside] * 4,
        out_specs=(inside,) * 3,
        scratch_shapes=[
            pltpu.VMEM((2, XS, tiles, 2, TILE, LANE), jnp.bfloat16),
            pltpu.VMEM((rows, width), jnp.bfloat16),
            pltpu.VMEM((rows, width), jnp.bfloat16),
            pltpu.VMEM((blocks, rows), jnp.int32),
            pltpu.VMEM((rows, blocks), jnp.int32),
            pltpu.VMEM((blocks, width), jnp.bfloat16),
            pltpu.VMEM((rows, width), jnp.float32),
            pltpu.VMEM((rows, width), jnp.float32),
            pltpu.VMEM((2, XS, tiles, 2, TILE, LANE), jnp.bfloat16),
            pltpu.VMEM((XS, tiles, 2, TILE, LANE), jnp.bfloat16),
            pltpu.VMEM((XS, tiles, 2, TILE, LANE), jnp.bfloat16),
            pltpu.VMEM((XS - 1, tiles, 2, TILE, LANE), jnp.bfloat16),
            pltpu.VMEM((rows, LANE), jnp.float32),
            pltpu.VMEM((tiles, 2, TILE, LANE), jnp.bfloat16),
            pltpu.VMEM((tiles, 2, TILE, LANE), jnp.bfloat16),
            dma((chunks, 2)),
            dma((2,)),
            *[dma((chunks,))] * 10,
            pltpu.VMEM((rows, LANE), jnp.float32),
            pltpu.SemaphoreType.REGULAR,
            pltpu.SemaphoreType.REGULAR,
        ],
        compiler_params=pltpu.CompilerParams(
            collective_id=0, has_side_effects=True, vmem_limit_bytes=24 << 20
        ),
        name="exchange",
    )(
        *(
            pltpu.with_memory_space_constraint(array, pltpu.HBM)
            for array in (
                inner2,
                anchor.reshape(rows, width),
                exponent.reshape(rows, blocks).T,
                momentum.reshape(rows, LANE),
            )
        )
    )

    anywhere = pl.BlockSpec(memory_space=pl.ANY)
    mixed, new_anchor, momentum_next = pl.pallas_call(
        flush,
        out_shape=results,
        in_specs=[anywhere] * 3,
        out_specs=(anywhere,) * 3,
        scratch_shapes=[dma((3,))],
        compiler_params=pltpu.CompilerParams(vmem_limit_bytes=16 << 20),
        name="flush",
    )(*inside_results)
    return (
        mixed.reshape(inner.shape),
        new_anchor.reshape(anchor.shape),
        momentum_next.reshape(momentum.shape),
    )


def solution(mesh):
    return jax.shard_map(
        on_device,
        mesh=mesh,
        in_specs=(
            P("rep", None, "fsdp", None),
            P(None, "fsdp", None),
            P("rep", None, "fsdp", None),
            P(None, "fsdp", "rep"),
        ),
        out_specs=(P("rep", None, "fsdp", None), P(None, "fsdp", None), P(None, "fsdp", "rep")),
        check_vma=False,
    )
```

```python
import functools

import jax
import jax.numpy as jnp
from jax import lax
from jax.experimental import pallas as pl
from jax.experimental.pallas import tpu as pltpu
from jax.sharding import PartitionSpec as P

MESH = pl.DeviceIdType.MESH
BLOCK = 32
LANE = 128
TILE = 16
XS = 4
REPS = 16
MINE, OTHER = 0.5, 0.7 * 1.9 / REPS
BOUNDS = ((0.25, 0.5), (0.75, 1.0), (1.25, 1.5), (1.75, 2.0), (2.5, 3.0), (3.5, 4.0), (5.0, 6.0))
CHUNKS = (1, 2, 3, 4, 3, 2, 1)
HOPS = len(CHUNKS) - 2
PLACES = tuple((c, x, h) for c in range(2) for x in range(XS) for h in range(2))
HEARD = 2 * XS - 1


def column_of(core, x, half):
    return (x * 4 + half * 2 + core) * LANE


PATIENT = 5
AHEAD = 2
SPANS = tuple((k, sum(CHUNKS[:k]), tiles) for k, tiles in enumerate(CHUNKS))


def exchange(
    inner,
    anchor,
    exponent,
    momentum,
    mixed,
    new_anchor,
    momentum_next,
    gathered,
    inner_v,
    anchor_v,
    exponent_v,
    power_rows,
    spread,
    scale_v,
    inverse_v,
    coded,
    pair_in,
    pairs,
    arrived,
    own_sum,
    z_out,
    z_in,
    load_sem,
    small_sem,
    core_send,
    core_recv,
    rs_send,
    rs_recv,
    z_send,
    z_recv,
    ag_send,
    ag_recv,
    out_send,
    out_recv,
    momentum_v,
    near_sem,
    far_sem,
):
    rep, fsdp = lax.axis_index("rep"), lax.axis_index("fsdp")
    x, half, core = rep // 4, (rep // 2) % 2, rep % 2
    late = jnp.logical_and(half == 1, fsdp % 8 >= PATIENT)
    own_column = pl.multiple_of(rep * LANE, LANE)
    other_column = pl.multiple_of((x * 4 + (1 - half) * 2 + core) * LANE, LANE)

    def beside(dx, there_core):
        there = lax.rem(x + dx, XS)
        return there, (there * 4 + half * 2 + there_core, fsdp)

    across = (x * 4 + (1 - half) * 2 + core, fsdp)

    partner = (x * 4 + half * 2 + 1 - core, fsdp)

    barrier = pltpu.get_barrier_semaphore()
    for dx in range(1, 4):
        hub = (lax.rem(x + dx, 4) * 4 + half * 2, fsdp)
        pl.semaphore_signal(barrier, inc=1, device_id=hub, device_id_type=MESH)

    @pl.when(core == 1)
    def _():
        pl.semaphore_signal(barrier, inc=1, device_id=partner, device_id_type=MESH)

    far = (x * 4 + (1 - half) * 2 + 1, fsdp)
    pl.semaphore_signal(barrier, inc=1, device_id=far, device_id_type=MESH)

    small = [
        pltpu.make_async_copy(exponent, exponent_v, small_sem.at[0]),
        pltpu.make_async_copy(momentum, momentum_v, small_sem.at[1]),
    ]
    small[0].start()
    loads = []
    for k, first, tiles in SPANS:
        rows = pl.ds(first * TILE, tiles * TILE)
        pair = (
            pltpu.make_async_copy(inner.at[rows], inner_v.at[rows], load_sem.at[k, 0]),
            pltpu.make_async_copy(anchor.at[rows], anchor_v.at[rows], load_sem.at[k, 1]),
        )
        for copy in pair:
            copy.start()
        loads.append(pair)
    small[1].start()

    width = anchor.shape[1]
    blocks = width // BLOCK
    block_of = lax.broadcasted_iota(jnp.int32, (blocks, width), 1) // BLOCK
    row_of = lax.broadcasted_iota(jnp.int32, (blocks, width), 0)
    spread[...] = jnp.where(block_of == row_of, 1.0, 0.0).astype(jnp.bfloat16)
    small[0].wait()
    power_rows[...] = exponent_v[...].T

    def start(source, destination, send, recv, device):
        pltpu.make_async_remote_copy(
            src_ref=source,
            dst_ref=destination,
            send_sem=send,
            recv_sem=recv,
            device_id=device,
            device_id_type=MESH,
        ).start()

    def wait(buffer, semaphore):
        pltpu.make_async_copy(buffer, buffer, semaphore).wait()

    def pass_pairs(k):
        _, first, tiles = SPANS[k]
        span = pl.ds(first, tiles)
        wait(pair_in.at[:, span], core_recv.at[k])

        def add(tile, carry):
            for place in range(XS):
                for h in range(2):
                    pairs[place, tile, h] = (
                        coded[core, place, tile, h].astype(jnp.float32)
                        + pair_in[place, tile, h].astype(jnp.float32)
                    ).astype(jnp.bfloat16)
            return carry

        lax.fori_loop(first, first + tiles, add, 0)
        for slot in (1, 0, 2):
            there, device = beside(slot + 1, core)
            start(pairs.at[there, span], arrived.at[slot, span], rs_send.at[k], rs_recv.at[k], device)

    for k, first, tiles in SPANS:
        rows = pl.ds(first * TILE, tiles * TILE)
        powers = power_rows[rows, :]
        scale, inverse = jnp.zeros(powers.shape, jnp.float32), jnp.zeros(powers.shape, jnp.float32)
        for power in (-1, 0, 1):
            scale = jnp.where(powers == power, jnp.float32(2.0**power), scale)
            inverse = jnp.where(powers == power, jnp.float32(2.0**-power), inverse)
        for value, target in ((scale, scale_v), (inverse, inverse_v)):
            target[rows, :] = jnp.dot(
                value.astype(jnp.bfloat16), spread[...], preferred_element_type=jnp.float32
            )
        for copy in loads[k]:
            copy.wait()

        def code(tile, carry):
            rows = pl.ds(pl.multiple_of(tile * TILE, TILE), TILE)
            for c, place, h in PLACES:
                columns = pl.ds(column_of(c, place, h), LANE)
                delta = anchor_v[rows, columns].astype(jnp.float32) - inner_v[
                    rows, columns
                ].astype(jnp.float32)
                magnitude = jnp.abs(delta) * inverse_v[rows, columns]
                scale = scale_v[rows, columns]
                level = jnp.zeros(delta.shape, jnp.float32)
                for bound, height in BOUNDS:
                    level = jnp.where(magnitude >= bound, jnp.float32(height), level)
                level = level * jnp.where(delta < 0, -scale, scale)
                coded[c, place, tile, h] = level.astype(jnp.bfloat16)
            return carry

        lax.fori_loop(first, first + tiles, code, 0)

        if k == 0:

            @pl.when(core == 0)
            def _():
                pl.semaphore_wait(barrier, HEARD)
                pl.semaphore_signal(near_sem, inc=1, device_id=partner, device_id_type=MESH)

            @pl.when(core == 1)
            def _():
                pl.semaphore_wait(near_sem, 1)

        span = pl.ds(first, tiles)
        start(
            coded.at[1 - core, :, span], pair_in.at[:, span], core_send.at[k], core_recv.at[k], partner
        )
        if k >= AHEAD:
            pass_pairs(k - AHEAD)
    for k in range(len(CHUNKS) - AHEAD, len(CHUNKS)):
        pass_pairs(k)

    @pl.when(core == 1)
    def _():
        pl.semaphore_wait(barrier, 2)
        pl.semaphore_signal(far_sem, inc=1, device_id=partner, device_id_type=MESH)

    @pl.when(core == 0)
    def _():
        pl.semaphore_wait(far_sem, 1)

    small[1].wait()
    for k, first, tiles in SPANS:
        span = pl.ds(first, tiles)
        wait(arrived.at[:, span], rs_recv.at[k])

        def add(tile, carry):
            rows = pl.ds(pl.multiple_of(tile * TILE, TILE), TILE)
            own = pairs[x, tile, half].astype(jnp.float32)
            other = pairs[x, tile, 1 - half].astype(jnp.float32)
            for slot in range(XS - 1):
                own = own + arrived[slot, tile, half].astype(jnp.float32)
                other = other + arrived[slot, tile, 1 - half].astype(jnp.float32)
            anchor_own = anchor_v[rows, pl.ds(own_column, LANE)].astype(jnp.float32)
            mine = MINE * anchor_own - OTHER * own - (0.7 * 0.81) * momentum_v[rows, :]
            own_sum[rows, :] = own
            z_out[tile, 0] = mine.astype(jnp.bfloat16)
            z_out[tile, 1] = other.astype(jnp.bfloat16)
            return carry

        lax.fori_loop(first, first + tiles, add, 0)
        if k == 0:

            @pl.when(late)
            def _():
                wait(z_in.at[span], z_recv.at[k])

        start(z_out.at[span], z_in.at[span], z_send.at[k], z_recv.at[k], across)

    def hand_over(k):
        _, first, tiles = SPANS[k]
        span = pl.ds(first, tiles)
        wait(arrived.at[:, span], ag_recv.at[k])
        whole = gathered.at[core, :, span]
        start(whole, whole, out_send.at[k], out_recv.at[k], partner)

    def mix(k):
        _, first, tiles = SPANS[k]
        span = pl.ds(first, tiles)
        if k >= HOPS:
            wait(arrived.at[:, span], ag_recv.at[k])
        wait(pair_in.at[:, span], out_recv.at[k])

        def part(tile, carry):
            rows = pl.ds(pl.multiple_of(tile * TILE, TILE), TILE)
            for c, place, h in PLACES:
                columns = pl.ds(column_of(c, place, h), LANE)
                new = gathered[c, place, tile, h]
                new_anchor[rows, columns] = new
                mixed[rows, columns] = (
                    0.5 * inner_v[rows, columns].astype(jnp.float32)
                    + 0.5 * new.astype(jnp.float32)
                ).astype(jnp.bfloat16)
            return carry

        lax.fori_loop(first, first + tiles, part, 0)

    for k, first, tiles in SPANS:
        span = pl.ds(first, tiles)
        if k == 0:

            @pl.when(jnp.logical_not(late))
            def _():
                wait(z_in.at[span], z_recv.at[k])

        else:
            wait(z_in.at[span], z_recv.at[k])

        def update(tile, carry):
            rows = pl.ds(pl.multiple_of(tile * TILE, TILE), TILE)

            def new(column, part, sums):
                wide = anchor_v[rows, pl.ds(column, LANE)].astype(jnp.float32)
                rest = (1.0 - MINE) * wide - OTHER * sums.astype(jnp.float32)
                return (part.astype(jnp.float32) + rest).astype(jnp.bfloat16)

            theirs = z_in[tile, 1]
            gathered[core, x, tile, half] = new(own_column, z_out[tile, 0], theirs)
            gathered[core, x, tile, 1 - half] = new(other_column, z_in[tile, 0], z_out[tile, 1])
            outer_grad = (own_sum[rows, :] + theirs.astype(jnp.float32)) * (1.0 / REPS)
            momentum_next[rows, :] = 0.9 * momentum_v[rows, :] + outer_grad
            return carry

        lax.fori_loop(first, first + tiles, update, 0)
        piece = gathered.at[core, x, span]
        for slot in (1, 0, 2):
            start(piece, piece, ag_send.at[k], ag_recv.at[k], beside(slot + 1, core)[1])
        if k >= HOPS:
            for slot in (1, 0, 2):
                other_core = beside(slot + 1, 1 - core)[1]
                start(piece, piece, out_send.at[k], out_recv.at[k], other_core)
            start(piece, piece, out_send.at[k], out_recv.at[k], partner)
    for k in range(HOPS):
        hand_over(k)
    for k in range(len(CHUNKS)):
        mix(k)

    for k, first, tiles in SPANS:
        span = pl.ds(first, tiles)
        wait(pair_in.at[:, span], core_send.at[k])
        wait(arrived.at[:, span], rs_send.at[k])
        wait(z_out.at[span], z_send.at[k])
        wait(arrived.at[:, span], ag_send.at[k])
        wait(pair_in.at[:, span], out_send.at[k])


def flush(*refs):
    results, outputs, sems = refs[:3], refs[3:6], refs[6]
    copies = [
        pltpu.make_async_copy(result, output, sems.at[i])
        for i, (result, output) in enumerate(zip(results, outputs))
    ]
    for copy in copies:
        copy.start()
    for copy in copies:
        copy.wait()


def on_device(inner, anchor, exponent, momentum):
    rows, width = anchor.shape[1:]
    tiles = rows // TILE
    blocks = exponent.shape[-1]
    inner2 = inner.reshape(rows, width)
    chunks = len(CHUNKS)
    outside = pl.BlockSpec(memory_space=pltpu.HBM)
    inside = pl.BlockSpec(memory_space=pltpu.VMEM)
    dma = pltpu.SemaphoreType.DMA
    results = (
        jax.ShapeDtypeStruct((rows, width), jnp.bfloat16),
        jax.ShapeDtypeStruct((rows, width), jnp.bfloat16),
        jax.ShapeDtypeStruct((rows, LANE), jnp.float32),
    )
    inside_results = pl.pallas_call(
        exchange,
        out_shape=results,
        in_specs=[outside] * 4,
        out_specs=(inside,) * 3,
        scratch_shapes=[
            pltpu.VMEM((2, XS, tiles, 2, TILE, LANE), jnp.bfloat16),
            pltpu.VMEM((rows, width), jnp.bfloat16),
            pltpu.VMEM((rows, width), jnp.bfloat16),
            pltpu.VMEM((blocks, rows), jnp.int32),
            pltpu.VMEM((rows, blocks), jnp.int32),
            pltpu.VMEM((blocks, width), jnp.bfloat16),
            pltpu.VMEM((rows, width), jnp.float32),
            pltpu.VMEM((rows, width), jnp.float32),
            pltpu.VMEM((2, XS, tiles, 2, TILE, LANE), jnp.bfloat16),
            pltpu.VMEM((XS, tiles, 2, TILE, LANE), jnp.bfloat16),
            pltpu.VMEM((XS, tiles, 2, TILE, LANE), jnp.bfloat16),
            pltpu.VMEM((XS - 1, tiles, 2, TILE, LANE), jnp.bfloat16),
            pltpu.VMEM((rows, LANE), jnp.float32),
            pltpu.VMEM((tiles, 2, TILE, LANE), jnp.bfloat16),
            pltpu.VMEM((tiles, 2, TILE, LANE), jnp.bfloat16),
            dma((chunks, 2)),
            dma((2,)),
            *[dma((chunks,))] * 10,
            pltpu.VMEM((rows, LANE), jnp.float32),
            pltpu.SemaphoreType.REGULAR,
            pltpu.SemaphoreType.REGULAR,
        ],
        compiler_params=pltpu.CompilerParams(
            collective_id=0, has_side_effects=True, vmem_limit_bytes=24 << 20
        ),
        name="exchange",
    )(
        *(
            pltpu.with_memory_space_constraint(array, pltpu.HBM)
            for array in (
                inner2,
                anchor.reshape(rows, width),
                exponent.reshape(rows, blocks).T,
                momentum.reshape(rows, LANE),
            )
        )
    )

    anywhere = pl.BlockSpec(memory_space=pl.ANY)
    mixed, new_anchor, momentum_next = pl.pallas_call(
        flush,
        out_shape=results,
        in_specs=[anywhere] * 3,
        out_specs=(anywhere,) * 3,
        scratch_shapes=[dma((3,))],
        compiler_params=pltpu.CompilerParams(vmem_limit_bytes=16 << 20),
        name="flush",
    )(*inside_results)
    return (
        mixed.reshape(inner.shape),
        new_anchor.reshape(anchor.shape),
        momentum_next.reshape(momentum.shape),
    )


def solution(mesh):
    return jax.shard_map(
        on_device,
        mesh=mesh,
        in_specs=(
            P("rep", None, "fsdp", None),
            P(None, "fsdp", None),
            P("rep", None, "fsdp", None),
            P(None, "fsdp", "rep"),
        ),
        out_specs=(P("rep", None, "fsdp", None), P(None, "fsdp", None), P(None, "fsdp", "rep")),
        check_vma=False,
    )
```

```python
import functools

import jax
import jax.numpy as jnp
from jax import lax
from jax.experimental import pallas as pl
from jax.experimental.pallas import tpu as pltpu
from jax.sharding import PartitionSpec as P

MESH = pl.DeviceIdType.MESH
BLOCK = 32
LANE = 128
TILE = 16
XS = 4
REPS = 16
MINE, OTHER = 0.5, 0.7 * 1.9 / REPS
BOUNDS = ((0.25, 0.5), (0.75, 1.0), (1.25, 1.5), (1.75, 2.0), (2.5, 3.0), (3.5, 4.0), (5.0, 6.0))
CHUNKS = (1, 2, 3, 4, 3, 2, 1)
HOPS = len(CHUNKS) - 2
PLACES = tuple((c, x, h) for c in range(2) for x in range(XS) for h in range(2))
HEARD = 2 * XS - 1


def column_of(core, x, half):
    return (x * 4 + half * 2 + core) * LANE


PATIENT = 5
DIRECT = 1
AHEAD = 2
SPANS = tuple((k, sum(CHUNKS[:k]), tiles) for k, tiles in enumerate(CHUNKS))


def exchange(
    inner,
    anchor,
    exponent,
    momentum,
    mixed,
    new_anchor,
    momentum_next,
    gathered,
    inner_v,
    anchor_v,
    exponent_v,
    power_rows,
    spread,
    scale_v,
    inverse_v,
    coded,
    pair_in,
    pairs,
    arrived,
    own_sum,
    z_out,
    z_in,
    load_sem,
    small_sem,
    core_send,
    core_recv,
    rs_send,
    rs_recv,
    z_send,
    z_recv,
    ag_send,
    ag_recv,
    out_send,
    out_recv,
    momentum_v,
    near_sem,
    far_sem,
):
    rep, fsdp = lax.axis_index("rep"), lax.axis_index("fsdp")
    x, half, core = rep // 4, (rep // 2) % 2, rep % 2
    late = jnp.logical_and(half == 1, fsdp % 8 >= PATIENT)
    own_column = pl.multiple_of(rep * LANE, LANE)
    other_column = pl.multiple_of((x * 4 + (1 - half) * 2 + core) * LANE, LANE)

    def beside(dx, there_core):
        there = lax.rem(x + dx, XS)
        return there, (there * 4 + half * 2 + there_core, fsdp)

    across = (x * 4 + (1 - half) * 2 + core, fsdp)

    partner = (x * 4 + half * 2 + 1 - core, fsdp)

    barrier = pltpu.get_barrier_semaphore()
    for dx in range(1, 4):
        hub = (lax.rem(x + dx, 4) * 4 + half * 2, fsdp)
        pl.semaphore_signal(barrier, inc=1, device_id=hub, device_id_type=MESH)

    @pl.when(core == 1)
    def _():
        pl.semaphore_signal(barrier, inc=1, device_id=partner, device_id_type=MESH)

    far = (x * 4 + (1 - half) * 2 + 1, fsdp)
    pl.semaphore_signal(barrier, inc=1, device_id=far, device_id_type=MESH)

    small = [
        pltpu.make_async_copy(exponent, exponent_v, small_sem.at[0]),
        pltpu.make_async_copy(momentum, momentum_v, small_sem.at[1]),
    ]
    small[0].start()
    loads = []
    for k, first, tiles in SPANS:
        rows = pl.ds(first * TILE, tiles * TILE)
        pair = (
            pltpu.make_async_copy(inner.at[rows], inner_v.at[rows], load_sem.at[k, 0]),
            pltpu.make_async_copy(anchor.at[rows], anchor_v.at[rows], load_sem.at[k, 1]),
        )
        for copy in pair:
            copy.start()
        loads.append(pair)
    small[1].start()

    width = anchor.shape[1]
    blocks = width // BLOCK
    block_of = lax.broadcasted_iota(jnp.int32, (blocks, width), 1) // BLOCK
    row_of = lax.broadcasted_iota(jnp.int32, (blocks, width), 0)
    spread[...] = jnp.where(block_of == row_of, 1.0, 0.0).astype(jnp.bfloat16)
    small[0].wait()
    power_rows[...] = exponent_v[...].T

    def start(source, destination, send, recv, device):
        pltpu.make_async_remote_copy(
            src_ref=source,
            dst_ref=destination,
            send_sem=send,
            recv_sem=recv,
            device_id=device,
            device_id_type=MESH,
        ).start()

    def wait(buffer, semaphore):
        pltpu.make_async_copy(buffer, buffer, semaphore).wait()

    def pass_pairs(k):
        _, first, tiles = SPANS[k]
        span = pl.ds(first, tiles)
        wait(pair_in.at[:, span], core_recv.at[k])

        def add(tile, carry):
            for place in range(XS):
                for h in range(2):
                    pairs[place, tile, h] = (
                        coded[core, place, tile, h].astype(jnp.float32)
                        + pair_in[place, tile, h].astype(jnp.float32)
                    ).astype(jnp.bfloat16)
            return carry

        lax.fori_loop(first, first + tiles, add, 0)
        for slot in (1, 0, 2):
            there, device = beside(slot + 1, core)
            start(pairs.at[there, span], arrived.at[slot, span], rs_send.at[k], rs_recv.at[k], device)

    for k, first, tiles in SPANS:
        rows = pl.ds(first * TILE, tiles * TILE)
        powers = power_rows[rows, :]
        scale, inverse = jnp.zeros(powers.shape, jnp.float32), jnp.zeros(powers.shape, jnp.float32)
        for power in (-1, 0, 1):
            scale = jnp.where(powers == power, jnp.float32(2.0**power), scale)
            inverse = jnp.where(powers == power, jnp.float32(2.0**-power), inverse)
        for value, target in ((scale, scale_v), (inverse, inverse_v)):
            target[rows, :] = jnp.dot(
                value.astype(jnp.bfloat16), spread[...], preferred_element_type=jnp.float32
            )
        for copy in loads[k]:
            copy.wait()

        def code(tile, carry):
            rows = pl.ds(pl.multiple_of(tile * TILE, TILE), TILE)
            for c, place, h in PLACES:
                columns = pl.ds(column_of(c, place, h), LANE)
                delta = anchor_v[rows, columns].astype(jnp.float32) - inner_v[
                    rows, columns
                ].astype(jnp.float32)
                magnitude = jnp.abs(delta) * inverse_v[rows, columns]
                scale = scale_v[rows, columns]
                level = jnp.zeros(delta.shape, jnp.float32)
                for bound, height in BOUNDS:
                    level = jnp.where(magnitude >= bound, jnp.float32(height), level)
                level = level * jnp.where(delta < 0, -scale, scale)
                coded[c, place, tile, h] = level.astype(jnp.bfloat16)
            return carry

        lax.fori_loop(first, first + tiles, code, 0)

        if k == 0:

            @pl.when(core == 0)
            def _():
                pl.semaphore_wait(barrier, HEARD)
                pl.semaphore_signal(near_sem, inc=1, device_id=partner, device_id_type=MESH)

            @pl.when(core == 1)
            def _():
                pl.semaphore_wait(near_sem, 1)

        span = pl.ds(first, tiles)
        if k < DIRECT:
            for slot in (1, 0, 2):
                there, device = beside(slot + 1, 1 - core)
                piece = coded.at[1 - core, there, span]
                start(piece, pair_in.at[x, span], core_send.at[k], core_recv.at[k], device)
                there, device = beside(slot + 1, core)
                piece = coded.at[core, there, span]
                start(piece, arrived.at[slot, span], rs_send.at[k], rs_recv.at[k], device)
            piece = coded.at[1 - core, x, span]
            start(piece, pair_in.at[x, span], core_send.at[k], core_recv.at[k], partner)
        else:
            pieces = coded.at[1 - core, :, span]
            start(pieces, pair_in.at[:, span], core_send.at[k], core_recv.at[k], partner)
        if k >= AHEAD + DIRECT:
            pass_pairs(k - AHEAD)
    for k in range(len(CHUNKS) - AHEAD, len(CHUNKS)):
        pass_pairs(k)

    @pl.when(core == 1)
    def _():
        pl.semaphore_wait(barrier, 2)
        pl.semaphore_signal(far_sem, inc=1, device_id=partner, device_id_type=MESH)

    @pl.when(core == 0)
    def _():
        pl.semaphore_wait(far_sem, 1)

    small[1].wait()
    for k, first, tiles in SPANS:
        span = pl.ds(first, tiles)
        wait(arrived.at[:, span], rs_recv.at[k])
        if k < DIRECT:
            wait(pair_in.at[:, span], core_recv.at[k])

        def add(tile, carry):
            rows = pl.ds(pl.multiple_of(tile * TILE, TILE), TILE)
            if k < DIRECT:
                own = coded[core, x, tile, half].astype(jnp.float32)
                other = coded[core, x, tile, 1 - half].astype(jnp.float32)
                for place in range(XS):
                    own = own + pair_in[place, tile, half].astype(jnp.float32)
                    other = other + pair_in[place, tile, 1 - half].astype(jnp.float32)
            else:
                own = pairs[x, tile, half].astype(jnp.float32)
                other = pairs[x, tile, 1 - half].astype(jnp.float32)
            for slot in range(XS - 1):
                own = own + arrived[slot, tile, half].astype(jnp.float32)
                other = other + arrived[slot, tile, 1 - half].astype(jnp.float32)
            anchor_own = anchor_v[rows, pl.ds(own_column, LANE)].astype(jnp.float32)
            mine = MINE * anchor_own - OTHER * own - (0.7 * 0.81) * momentum_v[rows, :]
            own_sum[rows, :] = own
            z_out[tile, 0] = mine.astype(jnp.bfloat16)
            z_out[tile, 1] = other.astype(jnp.bfloat16)
            return carry

        lax.fori_loop(first, first + tiles, add, 0)
        if k == 0:

            @pl.when(late)
            def _():
                wait(z_in.at[span], z_recv.at[k])

        start(z_out.at[span], z_in.at[span], z_send.at[k], z_recv.at[k], across)

    def hand_over(k):
        _, first, tiles = SPANS[k]
        span = pl.ds(first, tiles)
        wait(arrived.at[:, span], ag_recv.at[k])
        whole = gathered.at[core, :, span]
        start(whole, whole, out_send.at[k], out_recv.at[k], partner)

    def mix(k):
        _, first, tiles = SPANS[k]
        span = pl.ds(first, tiles)
        if k >= HOPS:
            wait(arrived.at[:, span], ag_recv.at[k])
        wait(pair_in.at[:, span], out_recv.at[k])

        def part(tile, carry):
            rows = pl.ds(pl.multiple_of(tile * TILE, TILE), TILE)
            for c, place, h in PLACES:
                columns = pl.ds(column_of(c, place, h), LANE)
                new = gathered[c, place, tile, h]
                new_anchor[rows, columns] = new
                mixed[rows, columns] = (
                    0.5 * inner_v[rows, columns].astype(jnp.float32)
                    + 0.5 * new.astype(jnp.float32)
                ).astype(jnp.bfloat16)
            return carry

        lax.fori_loop(first, first + tiles, part, 0)

    for k, first, tiles in SPANS:
        span = pl.ds(first, tiles)
        if k == 0:

            @pl.when(jnp.logical_not(late))
            def _():
                wait(z_in.at[span], z_recv.at[k])

        else:
            wait(z_in.at[span], z_recv.at[k])

        def update(tile, carry):
            rows = pl.ds(pl.multiple_of(tile * TILE, TILE), TILE)

            def new(column, part, sums):
                wide = anchor_v[rows, pl.ds(column, LANE)].astype(jnp.float32)
                rest = (1.0 - MINE) * wide - OTHER * sums.astype(jnp.float32)
                return (part.astype(jnp.float32) + rest).astype(jnp.bfloat16)

            theirs = z_in[tile, 1]
            gathered[core, x, tile, half] = new(own_column, z_out[tile, 0], theirs)
            gathered[core, x, tile, 1 - half] = new(other_column, z_in[tile, 0], z_out[tile, 1])
            outer_grad = (own_sum[rows, :] + theirs.astype(jnp.float32)) * (1.0 / REPS)
            momentum_next[rows, :] = 0.9 * momentum_v[rows, :] + outer_grad
            return carry

        lax.fori_loop(first, first + tiles, update, 0)
        piece = gathered.at[core, x, span]
        for slot in (1, 0, 2):
            start(piece, piece, ag_send.at[k], ag_recv.at[k], beside(slot + 1, core)[1])
        if k >= HOPS:
            for slot in (1, 0, 2):
                other_core = beside(slot + 1, 1 - core)[1]
                start(piece, piece, out_send.at[k], out_recv.at[k], other_core)
            start(piece, piece, out_send.at[k], out_recv.at[k], partner)
    for k in range(HOPS):
        hand_over(k)
    for k in range(len(CHUNKS)):
        mix(k)

    for k, first, tiles in SPANS:
        span = pl.ds(first, tiles)
        wait(pair_in.at[:, span], core_send.at[k])
        wait(arrived.at[:, span], rs_send.at[k])
        wait(z_out.at[span], z_send.at[k])
        wait(arrived.at[:, span], ag_send.at[k])
        wait(pair_in.at[:, span], out_send.at[k])


def flush(*refs):
    results, outputs, sems = refs[:3], refs[3:6], refs[6]
    copies = [
        pltpu.make_async_copy(result, output, sems.at[i])
        for i, (result, output) in enumerate(zip(results, outputs))
    ]
    for copy in copies:
        copy.start()
    for copy in copies:
        copy.wait()


def on_device(inner, anchor, exponent, momentum):
    rows, width = anchor.shape[1:]
    tiles = rows // TILE
    blocks = exponent.shape[-1]
    inner2 = inner.reshape(rows, width)
    chunks = len(CHUNKS)
    outside = pl.BlockSpec(memory_space=pltpu.HBM)
    inside = pl.BlockSpec(memory_space=pltpu.VMEM)
    dma = pltpu.SemaphoreType.DMA
    results = (
        jax.ShapeDtypeStruct((rows, width), jnp.bfloat16),
        jax.ShapeDtypeStruct((rows, width), jnp.bfloat16),
        jax.ShapeDtypeStruct((rows, LANE), jnp.float32),
    )
    inside_results = pl.pallas_call(
        exchange,
        out_shape=results,
        in_specs=[outside] * 4,
        out_specs=(inside,) * 3,
        scratch_shapes=[
            pltpu.VMEM((2, XS, tiles, 2, TILE, LANE), jnp.bfloat16),
            pltpu.VMEM((rows, width), jnp.bfloat16),
            pltpu.VMEM((rows, width), jnp.bfloat16),
            pltpu.VMEM((blocks, rows), jnp.int32),
            pltpu.VMEM((rows, blocks), jnp.int32),
            pltpu.VMEM((blocks, width), jnp.bfloat16),
            pltpu.VMEM((rows, width), jnp.float32),
            pltpu.VMEM((rows, width), jnp.float32),
            pltpu.VMEM((2, XS, tiles, 2, TILE, LANE), jnp.bfloat16),
            pltpu.VMEM((XS, tiles, 2, TILE, LANE), jnp.bfloat16),
            pltpu.VMEM((XS, tiles, 2, TILE, LANE), jnp.bfloat16),
            pltpu.VMEM((XS - 1, tiles, 2, TILE, LANE), jnp.bfloat16),
            pltpu.VMEM((rows, LANE), jnp.float32),
            pltpu.VMEM((tiles, 2, TILE, LANE), jnp.bfloat16),
            pltpu.VMEM((tiles, 2, TILE, LANE), jnp.bfloat16),
            dma((chunks, 2)),
            dma((2,)),
            *[dma((chunks,))] * 10,
            pltpu.VMEM((rows, LANE), jnp.float32),
            pltpu.SemaphoreType.REGULAR,
            pltpu.SemaphoreType.REGULAR,
        ],
        compiler_params=pltpu.CompilerParams(
            collective_id=0, has_side_effects=True, vmem_limit_bytes=24 << 20
        ),
        name="exchange",
    )(
        *(
            pltpu.with_memory_space_constraint(array, pltpu.HBM)
            for array in (
                inner2,
                anchor.reshape(rows, width),
                exponent.reshape(rows, blocks).T,
                momentum.reshape(rows, LANE),
            )
        )
    )

    anywhere = pl.BlockSpec(memory_space=pl.ANY)
    mixed, new_anchor, momentum_next = pl.pallas_call(
        flush,
        out_shape=results,
        in_specs=[anywhere] * 3,
        out_specs=(anywhere,) * 3,
        scratch_shapes=[dma((3,))],
        compiler_params=pltpu.CompilerParams(vmem_limit_bytes=16 << 20),
        name="flush",
    )(*inside_results)
    return (
        mixed.reshape(inner.shape),
        new_anchor.reshape(anchor.shape),
        momentum_next.reshape(momentum.shape),
    )


def solution(mesh):
    return jax.shard_map(
        on_device,
        mesh=mesh,
        in_specs=(
            P("rep", None, "fsdp", None),
            P(None, "fsdp", None),
            P("rep", None, "fsdp", None),
            P(None, "fsdp", "rep"),
        ),
        out_specs=(P("rep", None, "fsdp", None), P(None, "fsdp", None), P(None, "fsdp", "rep")),
        check_vma=False,
    )
```

```python
import functools

import jax
import jax.numpy as jnp
from jax import lax
from jax.experimental import pallas as pl
from jax.experimental.pallas import tpu as pltpu
from jax.sharding import PartitionSpec as P

MESH = pl.DeviceIdType.MESH
BLOCK = 32
LANE = 128
TILE = 16
XS = 4
REPS = 16
MINE, OTHER = 0.5, 0.7 * 1.9 / REPS
BOUNDS = ((0.25, 0.5), (0.75, 1.0), (1.25, 1.5), (1.75, 2.0), (2.5, 3.0), (3.5, 4.0), (5.0, 6.0))
CHUNKS = (1, 1, 2, 3, 3, 3, 2, 1)
HOPS = len(CHUNKS) - 2
PLACES = tuple((c, x, h) for c in range(2) for x in range(XS) for h in range(2))
HEARD = 2 * XS - 1


def column_of(core, x, half):
    return (x * 4 + half * 2 + core) * LANE


HELD = 4
DIRECT = 1
AHEAD = 2
SPANS = tuple((k, sum(CHUNKS[:k]), tiles) for k, tiles in enumerate(CHUNKS))


def exchange(
    inner,
    anchor,
    exponent,
    momentum,
    mixed,
    new_anchor,
    momentum_next,
    gathered,
    inner_v,
    anchor_v,
    exponent_v,
    power_rows,
    spread,
    scale_v,
    inverse_v,
    coded,
    pair_in,
    pairs,
    arrived,
    own_sum,
    z_out,
    z_in,
    load_sem,
    small_sem,
    core_send,
    core_recv,
    rs_send,
    rs_recv,
    z_send,
    z_recv,
    ag_send,
    ag_recv,
    out_send,
    out_recv,
    momentum_v,
    near_sem,
    far_sem,
):
    rep, fsdp = lax.axis_index("rep"), lax.axis_index("fsdp")
    x, half, core = rep // 4, (rep // 2) % 2, rep % 2
    pair = fsdp % 8
    late = jnp.logical_and(half == 1, jnp.logical_or(pair == 5, pair == 7))
    holds = jnp.logical_and(half == 1, pair == 6)
    own_column = pl.multiple_of(rep * LANE, LANE)
    other_column = pl.multiple_of((x * 4 + (1 - half) * 2 + core) * LANE, LANE)

    def beside(dx, there_core):
        there = lax.rem(x + dx, XS)
        return there, (there * 4 + half * 2 + there_core, fsdp)

    across = (x * 4 + (1 - half) * 2 + core, fsdp)

    partner = (x * 4 + half * 2 + 1 - core, fsdp)

    barrier = pltpu.get_barrier_semaphore()
    for dx in range(1, 4):
        hub = (lax.rem(x + dx, 4) * 4 + half * 2, fsdp)
        pl.semaphore_signal(barrier, inc=1, device_id=hub, device_id_type=MESH)

    @pl.when(core == 1)
    def _():
        pl.semaphore_signal(barrier, inc=1, device_id=partner, device_id_type=MESH)

    far = (x * 4 + (1 - half) * 2 + 1, fsdp)
    pl.semaphore_signal(barrier, inc=1, device_id=far, device_id_type=MESH)

    small = [
        pltpu.make_async_copy(exponent, exponent_v, small_sem.at[0]),
        pltpu.make_async_copy(momentum, momentum_v, small_sem.at[1]),
    ]
    small[0].start()
    loads = []
    for k, first, tiles in SPANS:
        rows = pl.ds(first * TILE, tiles * TILE)
        pair = (
            pltpu.make_async_copy(inner.at[rows], inner_v.at[rows], load_sem.at[k, 0]),
            pltpu.make_async_copy(anchor.at[rows], anchor_v.at[rows], load_sem.at[k, 1]),
        )
        for copy in pair:
            copy.start()
        loads.append(pair)
    small[1].start()

    width = anchor.shape[1]
    blocks = width // BLOCK
    block_of = lax.broadcasted_iota(jnp.int32, (blocks, width), 1) // BLOCK
    row_of = lax.broadcasted_iota(jnp.int32, (blocks, width), 0)
    spread[...] = jnp.where(block_of == row_of, 1.0, 0.0).astype(jnp.bfloat16)
    small[0].wait()
    power_rows[...] = exponent_v[...].T

    def start(source, destination, send, recv, device):
        pltpu.make_async_remote_copy(
            src_ref=source,
            dst_ref=destination,
            send_sem=send,
            recv_sem=recv,
            device_id=device,
            device_id_type=MESH,
        ).start()

    def wait(buffer, semaphore):
        pltpu.make_async_copy(buffer, buffer, semaphore).wait()

    def pass_pairs(k):
        _, first, tiles = SPANS[k]
        span = pl.ds(first, tiles)
        wait(pair_in.at[:, span], core_recv.at[k])

        def add(tile, carry):
            for place in range(XS):
                for h in range(2):
                    pairs[place, tile, h] = (
                        coded[core, place, tile, h].astype(jnp.float32)
                        + pair_in[place, tile, h].astype(jnp.float32)
                    ).astype(jnp.bfloat16)
            return carry

        lax.fori_loop(first, first + tiles, add, 0)
        for slot in (1, 0, 2):
            there, device = beside(slot + 1, core)
            start(pairs.at[there, span], arrived.at[slot, span], rs_send.at[k], rs_recv.at[k], device)

    for k, first, tiles in SPANS:
        rows = pl.ds(first * TILE, tiles * TILE)
        powers = power_rows[rows, :]
        scale, inverse = jnp.zeros(powers.shape, jnp.float32), jnp.zeros(powers.shape, jnp.float32)
        for power in (-1, 0, 1):
            scale = jnp.where(powers == power, jnp.float32(2.0**power), scale)
            inverse = jnp.where(powers == power, jnp.float32(2.0**-power), inverse)
        for value, target in ((scale, scale_v), (inverse, inverse_v)):
            target[rows, :] = jnp.dot(
                value.astype(jnp.bfloat16), spread[...], preferred_element_type=jnp.float32
            )
        for copy in loads[k]:
            copy.wait()

        def code(tile, carry):
            rows = pl.ds(pl.multiple_of(tile * TILE, TILE), TILE)
            for c, place, h in PLACES:
                columns = pl.ds(column_of(c, place, h), LANE)
                delta = anchor_v[rows, columns].astype(jnp.float32) - inner_v[
                    rows, columns
                ].astype(jnp.float32)
                magnitude = jnp.abs(delta) * inverse_v[rows, columns]
                scale = scale_v[rows, columns]
                level = jnp.zeros(delta.shape, jnp.float32)
                for bound, height in BOUNDS:
                    level = jnp.where(magnitude >= bound, jnp.float32(height), level)
                level = level * jnp.where(delta < 0, -scale, scale)
                coded[c, place, tile, h] = level.astype(jnp.bfloat16)
            return carry

        lax.fori_loop(first, first + tiles, code, 0)

        if k == 0:

            @pl.when(core == 0)
            def _():
                pl.semaphore_wait(barrier, HEARD)
                pl.semaphore_signal(near_sem, inc=1, device_id=partner, device_id_type=MESH)

            @pl.when(core == 1)
            def _():
                pl.semaphore_wait(near_sem, 1)

        span = pl.ds(first, tiles)
        if k < DIRECT:
            for slot in (1, 0, 2):
                there, device = beside(slot + 1, 1 - core)
                piece = coded.at[1 - core, there, span]
                start(piece, pair_in.at[x, span], core_send.at[k], core_recv.at[k], device)
                there, device = beside(slot + 1, core)
                piece = coded.at[core, there, span]
                start(piece, arrived.at[slot, span], rs_send.at[k], rs_recv.at[k], device)
            piece = coded.at[1 - core, x, span]
            start(piece, pair_in.at[x, span], core_send.at[k], core_recv.at[k], partner)
        else:
            pieces = coded.at[1 - core, :, span]
            start(pieces, pair_in.at[:, span], core_send.at[k], core_recv.at[k], partner)
        if k >= AHEAD + DIRECT:
            pass_pairs(k - AHEAD)
    for k in range(len(CHUNKS) - AHEAD, len(CHUNKS)):
        pass_pairs(k)

    @pl.when(core == 1)
    def _():
        pl.semaphore_wait(barrier, 2)
        pl.semaphore_signal(far_sem, inc=1, device_id=partner, device_id_type=MESH)

    @pl.when(core == 0)
    def _():
        pl.semaphore_wait(far_sem, 1)

    def cross(k):
        _, first, tiles = SPANS[k]
        span = pl.ds(first, tiles)
        start(z_out.at[span], z_in.at[span], z_send.at[k], z_recv.at[k], across)

    small[1].wait()
    for k, first, tiles in SPANS:
        span = pl.ds(first, tiles)
        wait(arrived.at[:, span], rs_recv.at[k])
        if k < DIRECT:
            wait(pair_in.at[:, span], core_recv.at[k])

        def add(tile, carry):
            rows = pl.ds(pl.multiple_of(tile * TILE, TILE), TILE)
            if k < DIRECT:
                own = coded[core, x, tile, half].astype(jnp.float32)
                other = coded[core, x, tile, 1 - half].astype(jnp.float32)
                for place in range(XS):
                    own = own + pair_in[place, tile, half].astype(jnp.float32)
                    other = other + pair_in[place, tile, 1 - half].astype(jnp.float32)
            else:
                own = pairs[x, tile, half].astype(jnp.float32)
                other = pairs[x, tile, 1 - half].astype(jnp.float32)
            for slot in range(XS - 1):
                own = own + arrived[slot, tile, half].astype(jnp.float32)
                other = other + arrived[slot, tile, 1 - half].astype(jnp.float32)
            anchor_own = anchor_v[rows, pl.ds(own_column, LANE)].astype(jnp.float32)
            mine = MINE * anchor_own - OTHER * own - (0.7 * 0.81) * momentum_v[rows, :]
            own_sum[rows, :] = own
            z_out[tile, 0] = mine.astype(jnp.bfloat16)
            z_out[tile, 1] = other.astype(jnp.bfloat16)
            return carry

        lax.fori_loop(first, first + tiles, add, 0)
        if k == 0:

            @pl.when(late)
            def _():
                wait(z_in.at[span], z_recv.at[k])

        if k == HELD:

            @pl.when(holds)
            def _():
                for held in range(HELD):
                    cross(held)

        if k < HELD:
            pl.when(jnp.logical_not(holds))(functools.partial(cross, k))
        else:
            cross(k)

    def hand_over(k):
        _, first, tiles = SPANS[k]
        span = pl.ds(first, tiles)
        wait(arrived.at[:, span], ag_recv.at[k])
        whole = gathered.at[core, :, span]
        start(whole, whole, out_send.at[k], out_recv.at[k], partner)

    def mix(k):
        _, first, tiles = SPANS[k]
        span = pl.ds(first, tiles)
        if k >= HOPS:
            wait(arrived.at[:, span], ag_recv.at[k])
        wait(pair_in.at[:, span], out_recv.at[k])

        def part(tile, carry):
            rows = pl.ds(pl.multiple_of(tile * TILE, TILE), TILE)
            for c, place, h in PLACES:
                columns = pl.ds(column_of(c, place, h), LANE)
                new = gathered[c, place, tile, h]
                new_anchor[rows, columns] = new
                mixed[rows, columns] = (
                    0.5 * inner_v[rows, columns].astype(jnp.float32)
                    + 0.5 * new.astype(jnp.float32)
                ).astype(jnp.bfloat16)
            return carry

        lax.fori_loop(first, first + tiles, part, 0)

    for k, first, tiles in SPANS:
        span = pl.ds(first, tiles)
        if k == 0:

            @pl.when(jnp.logical_not(late))
            def _():
                wait(z_in.at[span], z_recv.at[k])

        else:
            wait(z_in.at[span], z_recv.at[k])

        def update(tile, carry):
            rows = pl.ds(pl.multiple_of(tile * TILE, TILE), TILE)

            def new(column, part, sums):
                wide = anchor_v[rows, pl.ds(column, LANE)].astype(jnp.float32)
                rest = (1.0 - MINE) * wide - OTHER * sums.astype(jnp.float32)
                return (part.astype(jnp.float32) + rest).astype(jnp.bfloat16)

            theirs = z_in[tile, 1]
            gathered[core, x, tile, half] = new(own_column, z_out[tile, 0], theirs)
            gathered[core, x, tile, 1 - half] = new(other_column, z_in[tile, 0], z_out[tile, 1])
            outer_grad = (own_sum[rows, :] + theirs.astype(jnp.float32)) * (1.0 / REPS)
            momentum_next[rows, :] = 0.9 * momentum_v[rows, :] + outer_grad
            return carry

        lax.fori_loop(first, first + tiles, update, 0)
        piece = gathered.at[core, x, span]
        for slot in (1, 0, 2):
            start(piece, piece, ag_send.at[k], ag_recv.at[k], beside(slot + 1, core)[1])
        if k >= HOPS:
            for slot in (1, 0, 2):
                other_core = beside(slot + 1, 1 - core)[1]
                start(piece, piece, out_send.at[k], out_recv.at[k], other_core)
            start(piece, piece, out_send.at[k], out_recv.at[k], partner)
    for k in range(HOPS):
        hand_over(k)
    for k in range(len(CHUNKS)):
        mix(k)

    for k, first, tiles in SPANS:
        span = pl.ds(first, tiles)
        wait(pair_in.at[:, span], core_send.at[k])
        wait(arrived.at[:, span], rs_send.at[k])
        wait(z_out.at[span], z_send.at[k])
        wait(arrived.at[:, span], ag_send.at[k])
        wait(pair_in.at[:, span], out_send.at[k])


def flush(*refs):
    results, outputs, sems = refs[:3], refs[3:6], refs[6]
    copies = [
        pltpu.make_async_copy(result, output, sems.at[i])
        for i, (result, output) in enumerate(zip(results, outputs))
    ]
    for copy in copies:
        copy.start()
    for copy in copies:
        copy.wait()


def on_device(inner, anchor, exponent, momentum):
    rows, width = anchor.shape[1:]
    tiles = rows // TILE
    blocks = exponent.shape[-1]
    inner2 = inner.reshape(rows, width)
    chunks = len(CHUNKS)
    outside = pl.BlockSpec(memory_space=pltpu.HBM)
    inside = pl.BlockSpec(memory_space=pltpu.VMEM)
    dma = pltpu.SemaphoreType.DMA
    results = (
        jax.ShapeDtypeStruct((rows, width), jnp.bfloat16),
        jax.ShapeDtypeStruct((rows, width), jnp.bfloat16),
        jax.ShapeDtypeStruct((rows, LANE), jnp.float32),
    )
    inside_results = pl.pallas_call(
        exchange,
        out_shape=results,
        in_specs=[outside] * 4,
        out_specs=(inside,) * 3,
        scratch_shapes=[
            pltpu.VMEM((2, XS, tiles, 2, TILE, LANE), jnp.bfloat16),
            pltpu.VMEM((rows, width), jnp.bfloat16),
            pltpu.VMEM((rows, width), jnp.bfloat16),
            pltpu.VMEM((blocks, rows), jnp.int32),
            pltpu.VMEM((rows, blocks), jnp.int32),
            pltpu.VMEM((blocks, width), jnp.bfloat16),
            pltpu.VMEM((rows, width), jnp.float32),
            pltpu.VMEM((rows, width), jnp.float32),
            pltpu.VMEM((2, XS, tiles, 2, TILE, LANE), jnp.bfloat16),
            pltpu.VMEM((XS, tiles, 2, TILE, LANE), jnp.bfloat16),
            pltpu.VMEM((XS, tiles, 2, TILE, LANE), jnp.bfloat16),
            pltpu.VMEM((XS - 1, tiles, 2, TILE, LANE), jnp.bfloat16),
            pltpu.VMEM((rows, LANE), jnp.float32),
            pltpu.VMEM((tiles, 2, TILE, LANE), jnp.bfloat16),
            pltpu.VMEM((tiles, 2, TILE, LANE), jnp.bfloat16),
            dma((chunks, 2)),
            dma((2,)),
            *[dma((chunks,))] * 10,
            pltpu.VMEM((rows, LANE), jnp.float32),
            pltpu.SemaphoreType.REGULAR,
            pltpu.SemaphoreType.REGULAR,
        ],
        compiler_params=pltpu.CompilerParams(
            collective_id=0, has_side_effects=True, vmem_limit_bytes=24 << 20
        ),
        name="exchange",
    )(
        *(
            pltpu.with_memory_space_constraint(array, pltpu.HBM)
            for array in (
                inner2,
                anchor.reshape(rows, width),
                exponent.reshape(rows, blocks).T,
                momentum.reshape(rows, LANE),
            )
        )
    )

    anywhere = pl.BlockSpec(memory_space=pl.ANY)
    mixed, new_anchor, momentum_next = pl.pallas_call(
        flush,
        out_shape=results,
        in_specs=[anywhere] * 3,
        out_specs=(anywhere,) * 3,
        scratch_shapes=[dma((3,))],
        compiler_params=pltpu.CompilerParams(vmem_limit_bytes=16 << 20),
        name="flush",
    )(*inside_results)
    return (
        mixed.reshape(inner.shape),
        new_anchor.reshape(anchor.shape),
        momentum_next.reshape(momentum.shape),
    )


def solution(mesh):
    return jax.shard_map(
        on_device,
        mesh=mesh,
        in_specs=(
            P("rep", None, "fsdp", None),
            P(None, "fsdp", None),
            P("rep", None, "fsdp", None),
            P(None, "fsdp", "rep"),
        ),
        out_specs=(P("rep", None, "fsdp", None), P(None, "fsdp", None), P(None, "fsdp", "rep")),
        check_vma=False,
    )
```

```python
import functools

import jax
import jax.numpy as jnp
from jax import lax
from jax.experimental import pallas as pl
from jax.experimental.pallas import tpu as pltpu
from jax.sharding import PartitionSpec as P

MESH = pl.DeviceIdType.MESH
BLOCK = 32
LANE = 128
TILE = 16
XS = 4
REPS = 16
MINE, OTHER = 0.5, 0.7 * 1.9 / REPS
BOUNDS = ((0.25, 0.5), (0.75, 1.0), (1.25, 1.5), (1.75, 2.0), (2.5, 3.0), (3.5, 4.0), (5.0, 6.0))
CHUNKS = (1, 1, 2, 3, 3, 3, 2, 1)
HOPS = len(CHUNKS) - 2
PLACES = tuple((c, x, h) for c in range(2) for x in range(XS) for h in range(2))
HEARD = 2 * XS - 1


def column_of(core, x, half):
    return (x * 4 + half * 2 + core) * LANE


HELD = 4
DIRECT = 1
AHEAD = 2
SPANS = tuple((k, sum(CHUNKS[:k]), tiles) for k, tiles in enumerate(CHUNKS))


def exchange(
    inner,
    anchor,
    exponent,
    momentum,
    mixed,
    new_anchor,
    momentum_next,
    gathered,
    inner_v,
    anchor_v,
    exponent_v,
    power_rows,
    spread,
    scale_v,
    inverse_v,
    coded,
    pair_in,
    pairs,
    arrived,
    own_sum,
    z_out,
    z_in,
    load_sem,
    small_sem,
    core_send,
    core_recv,
    rs_send,
    rs_recv,
    z_send,
    z_recv,
    ag_send,
    ag_recv,
    out_send,
    out_recv,
    momentum_v,
    near_sem,
    far_sem,
):
    rep, fsdp = lax.axis_index("rep"), lax.axis_index("fsdp")
    x, half, core = rep // 4, (rep // 2) % 2, rep % 2
    pair = fsdp % 8
    late = jnp.logical_and(half == 1, jnp.logical_or(pair == 5, pair == 7))
    held_pair = jnp.logical_or(pair == 6, jnp.logical_or(pair == 3, pair == 4))
    holds = jnp.logical_and(half == 1, held_pair)
    own_column = pl.multiple_of(rep * LANE, LANE)
    other_column = pl.multiple_of((x * 4 + (1 - half) * 2 + core) * LANE, LANE)

    def beside(dx, there_core):
        there = lax.rem(x + dx, XS)
        return there, (there * 4 + half * 2 + there_core, fsdp)

    across = (x * 4 + (1 - half) * 2 + core, fsdp)

    partner = (x * 4 + half * 2 + 1 - core, fsdp)

    barrier = pltpu.get_barrier_semaphore()
    for dx in range(1, 4):
        hub = (lax.rem(x + dx, 4) * 4 + half * 2, fsdp)
        pl.semaphore_signal(barrier, inc=1, device_id=hub, device_id_type=MESH)

    @pl.when(core == 1)
    def _():
        pl.semaphore_signal(barrier, inc=1, device_id=partner, device_id_type=MESH)

    far = (x * 4 + (1 - half) * 2 + 1, fsdp)
    pl.semaphore_signal(barrier, inc=1, device_id=far, device_id_type=MESH)

    small = [
        pltpu.make_async_copy(exponent, exponent_v, small_sem.at[0]),
        pltpu.make_async_copy(momentum, momentum_v, small_sem.at[1]),
    ]
    small[0].start()
    loads = []
    for k, first, tiles in SPANS:
        rows = pl.ds(first * TILE, tiles * TILE)
        pair = (
            pltpu.make_async_copy(inner.at[rows], inner_v.at[rows], load_sem.at[k, 0]),
            pltpu.make_async_copy(anchor.at[rows], anchor_v.at[rows], load_sem.at[k, 1]),
        )
        for copy in pair:
            copy.start()
        loads.append(pair)
    small[1].start()

    width = anchor.shape[1]
    blocks = width // BLOCK
    block_of = lax.broadcasted_iota(jnp.int32, (blocks, width), 1) // BLOCK
    row_of = lax.broadcasted_iota(jnp.int32, (blocks, width), 0)
    spread[...] = jnp.where(block_of == row_of, 1.0, 0.0).astype(jnp.bfloat16)
    small[0].wait()
    power_rows[...] = exponent_v[...].T

    def start(source, destination, send, recv, device):
        pltpu.make_async_remote_copy(
            src_ref=source,
            dst_ref=destination,
            send_sem=send,
            recv_sem=recv,
            device_id=device,
            device_id_type=MESH,
        ).start()

    def wait(buffer, semaphore):
        pltpu.make_async_copy(buffer, buffer, semaphore).wait()

    def pass_pairs(k):
        _, first, tiles = SPANS[k]
        span = pl.ds(first, tiles)
        wait(pair_in.at[:, span], core_recv.at[k])

        def add(tile, carry):
            for place in range(XS):
                for h in range(2):
                    pairs[place, tile, h] = (
                        coded[core, place, tile, h].astype(jnp.float32)
                        + pair_in[place, tile, h].astype(jnp.float32)
                    ).astype(jnp.bfloat16)
            return carry

        lax.fori_loop(first, first + tiles, add, 0)
        for slot in (1, 0, 2):
            there, device = beside(slot + 1, core)
            start(pairs.at[there, span], arrived.at[slot, span], rs_send.at[k], rs_recv.at[k], device)

    for k, first, tiles in SPANS:
        rows = pl.ds(first * TILE, tiles * TILE)
        powers = power_rows[rows, :]
        scale, inverse = jnp.zeros(powers.shape, jnp.float32), jnp.zeros(powers.shape, jnp.float32)
        for power in (-1, 0, 1):
            scale = jnp.where(powers == power, jnp.float32(2.0**power), scale)
            inverse = jnp.where(powers == power, jnp.float32(2.0**-power), inverse)
        for value, target in ((scale, scale_v), (inverse, inverse_v)):
            target[rows, :] = jnp.dot(
                value.astype(jnp.bfloat16), spread[...], preferred_element_type=jnp.float32
            )
        for copy in loads[k]:
            copy.wait()

        def code(tile, carry):
            rows = pl.ds(pl.multiple_of(tile * TILE, TILE), TILE)
            for c, place, h in PLACES:
                columns = pl.ds(column_of(c, place, h), LANE)
                delta = anchor_v[rows, columns].astype(jnp.float32) - inner_v[
                    rows, columns
                ].astype(jnp.float32)
                magnitude = jnp.abs(delta) * inverse_v[rows, columns]
                scale = scale_v[rows, columns]
                level = jnp.zeros(delta.shape, jnp.float32)
                for bound, height in BOUNDS:
                    level = jnp.where(magnitude >= bound, jnp.float32(height), level)
                level = level * jnp.where(delta < 0, -scale, scale)
                coded[c, place, tile, h] = level.astype(jnp.bfloat16)
            return carry

        lax.fori_loop(first, first + tiles, code, 0)

        if k == 0:

            @pl.when(core == 0)
            def _():
                pl.semaphore_wait(barrier, HEARD)
                pl.semaphore_signal(near_sem, inc=1, device_id=partner, device_id_type=MESH)

            @pl.when(core == 1)
            def _():
                pl.semaphore_wait(near_sem, 1)

        span = pl.ds(first, tiles)
        if k < DIRECT:
            for slot in (1, 0, 2):
                there, device = beside(slot + 1, 1 - core)
                piece = coded.at[1 - core, there, span]
                start(piece, pair_in.at[x, span], core_send.at[k], core_recv.at[k], device)
                there, device = beside(slot + 1, core)
                piece = coded.at[core, there, span]
                start(piece, arrived.at[slot, span], rs_send.at[k], rs_recv.at[k], device)
            piece = coded.at[1 - core, x, span]
            start(piece, pair_in.at[x, span], core_send.at[k], core_recv.at[k], partner)
        else:
            pieces = coded.at[1 - core, :, span]
            start(pieces, pair_in.at[:, span], core_send.at[k], core_recv.at[k], partner)
        if k >= AHEAD + DIRECT:
            pass_pairs(k - AHEAD)
    for k in range(len(CHUNKS) - AHEAD, len(CHUNKS)):
        pass_pairs(k)

    @pl.when(core == 1)
    def _():
        pl.semaphore_wait(barrier, 2)
        pl.semaphore_signal(far_sem, inc=1, device_id=partner, device_id_type=MESH)

    @pl.when(core == 0)
    def _():
        pl.semaphore_wait(far_sem, 1)

    def cross(k):
        _, first, tiles = SPANS[k]
        span = pl.ds(first, tiles)
        start(z_out.at[span], z_in.at[span], z_send.at[k], z_recv.at[k], across)

    small[1].wait()
    for k, first, tiles in SPANS:
        span = pl.ds(first, tiles)
        wait(arrived.at[:, span], rs_recv.at[k])
        if k < DIRECT:
            wait(pair_in.at[:, span], core_recv.at[k])

        def add(tile, carry):
            rows = pl.ds(pl.multiple_of(tile * TILE, TILE), TILE)
            if k < DIRECT:
                own = coded[core, x, tile, half].astype(jnp.float32)
                other = coded[core, x, tile, 1 - half].astype(jnp.float32)
                for place in range(XS):
                    own = own + pair_in[place, tile, half].astype(jnp.float32)
                    other = other + pair_in[place, tile, 1 - half].astype(jnp.float32)
            else:
                own = pairs[x, tile, half].astype(jnp.float32)
                other = pairs[x, tile, 1 - half].astype(jnp.float32)
            for slot in range(XS - 1):
                own = own + arrived[slot, tile, half].astype(jnp.float32)
                other = other + arrived[slot, tile, 1 - half].astype(jnp.float32)
            anchor_own = anchor_v[rows, pl.ds(own_column, LANE)].astype(jnp.float32)
            mine = MINE * anchor_own - OTHER * own - (0.7 * 0.81) * momentum_v[rows, :]
            own_sum[rows, :] = own
            z_out[tile, 0] = mine.astype(jnp.bfloat16)
            z_out[tile, 1] = other.astype(jnp.bfloat16)
            return carry

        lax.fori_loop(first, first + tiles, add, 0)
        if k == 0:

            @pl.when(late)
            def _():
                wait(z_in.at[span], z_recv.at[k])

        if k == HELD:

            @pl.when(holds)
            def _():
                for held in range(HELD):
                    cross(held)

        if k < HELD:
            pl.when(jnp.logical_not(holds))(functools.partial(cross, k))
        else:
            cross(k)

    def hand_over(k):
        _, first, tiles = SPANS[k]
        span = pl.ds(first, tiles)
        wait(arrived.at[:, span], ag_recv.at[k])
        whole = gathered.at[core, :, span]
        start(whole, whole, out_send.at[k], out_recv.at[k], partner)

    def mix(k):
        _, first, tiles = SPANS[k]
        span = pl.ds(first, tiles)
        if k >= HOPS:
            wait(arrived.at[:, span], ag_recv.at[k])
        wait(pair_in.at[:, span], out_recv.at[k])

        def part(tile, carry):
            rows = pl.ds(pl.multiple_of(tile * TILE, TILE), TILE)
            for c, place, h in PLACES:
                columns = pl.ds(column_of(c, place, h), LANE)
                new = gathered[c, place, tile, h]
                new_anchor[rows, columns] = new
                mixed[rows, columns] = (
                    0.5 * inner_v[rows, columns].astype(jnp.float32)
                    + 0.5 * new.astype(jnp.float32)
                ).astype(jnp.bfloat16)
            return carry

        lax.fori_loop(first, first + tiles, part, 0)

    for k, first, tiles in SPANS:
        span = pl.ds(first, tiles)
        if k == 0:

            @pl.when(jnp.logical_not(late))
            def _():
                wait(z_in.at[span], z_recv.at[k])

        else:
            wait(z_in.at[span], z_recv.at[k])

        def update(tile, carry):
            rows = pl.ds(pl.multiple_of(tile * TILE, TILE), TILE)

            def new(column, part, sums):
                wide = anchor_v[rows, pl.ds(column, LANE)].astype(jnp.float32)
                rest = (1.0 - MINE) * wide - OTHER * sums.astype(jnp.float32)
                return (part.astype(jnp.float32) + rest).astype(jnp.bfloat16)

            theirs = z_in[tile, 1]
            gathered[core, x, tile, half] = new(own_column, z_out[tile, 0], theirs)
            gathered[core, x, tile, 1 - half] = new(other_column, z_in[tile, 0], z_out[tile, 1])
            outer_grad = (own_sum[rows, :] + theirs.astype(jnp.float32)) * (1.0 / REPS)
            momentum_next[rows, :] = 0.9 * momentum_v[rows, :] + outer_grad
            return carry

        lax.fori_loop(first, first + tiles, update, 0)
        piece = gathered.at[core, x, span]
        for slot in (1, 0, 2):
            start(piece, piece, ag_send.at[k], ag_recv.at[k], beside(slot + 1, core)[1])
        if k >= HOPS:
            for slot in (1, 0, 2):
                other_core = beside(slot + 1, 1 - core)[1]
                start(piece, piece, out_send.at[k], out_recv.at[k], other_core)
            start(piece, piece, out_send.at[k], out_recv.at[k], partner)
    for k in range(HOPS):
        hand_over(k)
    for k in range(len(CHUNKS)):
        mix(k)

    for k, first, tiles in SPANS:
        span = pl.ds(first, tiles)
        wait(pair_in.at[:, span], core_send.at[k])
        wait(arrived.at[:, span], rs_send.at[k])
        wait(z_out.at[span], z_send.at[k])
        wait(arrived.at[:, span], ag_send.at[k])
        wait(pair_in.at[:, span], out_send.at[k])


def flush(*refs):
    results, outputs, sems = refs[:3], refs[3:6], refs[6]
    copies = [
        pltpu.make_async_copy(result, output, sems.at[i])
        for i, (result, output) in enumerate(zip(results, outputs))
    ]
    for copy in copies:
        copy.start()
    for copy in copies:
        copy.wait()


def on_device(inner, anchor, exponent, momentum):
    rows, width = anchor.shape[1:]
    tiles = rows // TILE
    blocks = exponent.shape[-1]
    inner2 = inner.reshape(rows, width)
    chunks = len(CHUNKS)
    outside = pl.BlockSpec(memory_space=pltpu.HBM)
    inside = pl.BlockSpec(memory_space=pltpu.VMEM)
    dma = pltpu.SemaphoreType.DMA
    results = (
        jax.ShapeDtypeStruct((rows, width), jnp.bfloat16),
        jax.ShapeDtypeStruct((rows, width), jnp.bfloat16),
        jax.ShapeDtypeStruct((rows, LANE), jnp.float32),
    )
    inside_results = pl.pallas_call(
        exchange,
        out_shape=results,
        in_specs=[outside] * 4,
        out_specs=(inside,) * 3,
        scratch_shapes=[
            pltpu.VMEM((2, XS, tiles, 2, TILE, LANE), jnp.bfloat16),
            pltpu.VMEM((rows, width), jnp.bfloat16),
            pltpu.VMEM((rows, width), jnp.bfloat16),
            pltpu.VMEM((blocks, rows), jnp.int32),
            pltpu.VMEM((rows, blocks), jnp.int32),
            pltpu.VMEM((blocks, width), jnp.bfloat16),
            pltpu.VMEM((rows, width), jnp.float32),
            pltpu.VMEM((rows, width), jnp.float32),
            pltpu.VMEM((2, XS, tiles, 2, TILE, LANE), jnp.bfloat16),
            pltpu.VMEM((XS, tiles, 2, TILE, LANE), jnp.bfloat16),
            pltpu.VMEM((XS, tiles, 2, TILE, LANE), jnp.bfloat16),
            pltpu.VMEM((XS - 1, tiles, 2, TILE, LANE), jnp.bfloat16),
            pltpu.VMEM((rows, LANE), jnp.float32),
            pltpu.VMEM((tiles, 2, TILE, LANE), jnp.bfloat16),
            pltpu.VMEM((tiles, 2, TILE, LANE), jnp.bfloat16),
            dma((chunks, 2)),
            dma((2,)),
            *[dma((chunks,))] * 10,
            pltpu.VMEM((rows, LANE), jnp.float32),
            pltpu.SemaphoreType.REGULAR,
            pltpu.SemaphoreType.REGULAR,
        ],
        compiler_params=pltpu.CompilerParams(
            collective_id=0, has_side_effects=True, vmem_limit_bytes=24 << 20
        ),
        name="exchange",
    )(
        *(
            pltpu.with_memory_space_constraint(array, pltpu.HBM)
            for array in (
                inner2,
                anchor.reshape(rows, width),
                exponent.reshape(rows, blocks).T,
                momentum.reshape(rows, LANE),
            )
        )
    )

    anywhere = pl.BlockSpec(memory_space=pl.ANY)
    mixed, new_anchor, momentum_next = pl.pallas_call(
        flush,
        out_shape=results,
        in_specs=[anywhere] * 3,
        out_specs=(anywhere,) * 3,
        scratch_shapes=[dma((3,))],
        compiler_params=pltpu.CompilerParams(vmem_limit_bytes=16 << 20),
        name="flush",
    )(*inside_results)
    return (
        mixed.reshape(inner.shape),
        new_anchor.reshape(anchor.shape),
        momentum_next.reshape(momentum.shape),
    )


def solution(mesh):
    return jax.shard_map(
        on_device,
        mesh=mesh,
        in_specs=(
            P("rep", None, "fsdp", None),
            P(None, "fsdp", None),
            P("rep", None, "fsdp", None),
            P(None, "fsdp", "rep"),
        ),
        out_specs=(P("rep", None, "fsdp", None), P(None, "fsdp", None), P(None, "fsdp", "rep")),
        check_vma=False,
    )
```
